256 devices in a mesh: clip: 16 (over x, y), tile: 16 (over z, core).
Axes of the slice: x: 4, y: 4, z: 8, core: 2. Of those that a mesh axis runs over, the one named last changes fastest.
Arguments:
- decoder_input: bfloat16 [16, 16, 32, 96, 128], P('clip', 'tile'), may hold values from -210 to 210
- reward_grad: bfloat16 [16, 32, 32, 96, 128], P('clip', 'tile'), may hold values from -6 to 6
- reward_owner: int32 [16, 16, 1], P('clip'), may hold values from 0 to 15; in each aligned block of 16 rows (0 to 15, 16 to 31, ..., all dimensions but the last counted through in order) at most 2 rows name the same one
- scored_frame: int32 [16, 16], P('clip'), may hold values from 0 to 15
- first_gain: float32 [96], replicated, may hold values from 0.1 to 1.9
- second_gain: float32 [96], replicated, may hold values from 0.1 to 1.9
- first_kernel: bfloat16 [3, 3, 3, 96, 96], replicated, may hold values from -0.125 to 0.125
- second_kernel: bfloat16 [3, 3, 3, 96, 96], replicated, may hold values from -0.125 to 0.125
Outputs:
- feature_grad: bfloat16 [16, 16, 32, 96, 128], P('clip', 'tile')
- first_kernel_grad: float32 [3, 3, 3, 96, 96], replicated
- second_kernel_grad: float32 [3, 3, 3, 96, 96], replicated
The draws below stay inside these ranges and needn't reach their ends.
Inputs may be any that keep to these rules, and one draw needn't show every extreme that they name: `reward_owner`: in each clip at most 2 scored entries share a reward device, and in every draw some device of some clip holds exactly 2; every slot that no entry names is ignored.
All inputs are finite; a program needn't handle non-finite values.
Results may differ from the reference program's by a relative error of at most 0.0073.
Values may be sent and summed in bfloat16 or wider, within the bound.
A program may use at most 128 MiB of HBM per device.

```python
import math
import jax
import jax.numpy as jnp
import numpy as np
from jax import lax

CHANNELS = 96
WIDTH = 128
SLOTS = 2
FRAMES = 16
ROWS = 32
CLIPS = 16
REWARD_SLOTS = 32
N_TILE = 16


def draw_decoder_input(key, part):
    key = jax.random.fold_in(key, 17)
    entry_key, row_key, channel_key, column_key = jax.random.split(key, 4)
    full_shape = (CLIPS, FRAMES, ROWS, CHANNELS, WIDTH)
    height = jnp.arange(ROWS, dtype=jnp.float32) / max(ROWS - 1, 1)
    rising = 3.0 ** (height - 0.5)
    row_scale = rising[None, None, :] * 10.0 ** jax.random.uniform(row_key, (CLIPS, FRAMES, ROWS), jnp.float32, -0.3, 0.3)
    column_scale = 10.0 ** jax.random.uniform(column_key, (CLIPS, 1, 1, 1, WIDTH), jnp.float32, -0.5, 0.5)
    entries = jnp.clip(jax.random.normal(entry_key, full_shape, jnp.float32), -6.0, 6.0)
    channel_scale = 10.0 ** jax.random.uniform(channel_key, (CLIPS, 1, 1, CHANNELS, 1), jnp.float32, -0.5, 0.5)
    values = entries * row_scale[:, :, :, None, None] * channel_scale * column_scale
    return values.astype(jnp.bfloat16)


def plant(drawn, own_key, smallest, largest):
    index_at = [jax.random.randint(jax.random.fold_in(own_key, axis), (), 0, length) for axis, length in enumerate(drawn.shape)]
    main_axis = drawn.shape.index(max(drawn.shape))
    beside = index_at[:main_axis] + [(index_at[main_axis] + 1) % drawn.shape[main_axis]] + index_at[main_axis + 1:]
    return drawn.at[tuple(index_at)].set(smallest).at[tuple(beside)].set(largest)


def level_of(stream_key, extent, cuts, low, top_value):
    def one(axis_at, blocks):
        draws = jax.random.uniform(jax.random.fold_in(jax.random.fold_in(stream_key, 6), axis_at), (blocks,), jnp.float32, low / len(cuts), top_value / len(cuts))
        return jnp.repeat(jnp.exp(draws), extent[axis_at] // blocks).reshape((-1,) + (1,) * (len(extent) - axis_at - 1))

    gain = one(*cuts[0])
    for cut in cuts[1:]:
        gain = gain * one(*cut)
    return gain


def shared_out(key, own, number, rows, number_of, top, reach, skew):
    order = jax.random.permutation(key, number_of)
    packed, usual = portions_of(number_of, rows * top, reach, skew, True), portions_of(number_of, rows * top, reach, skew, False)
    places = jnp.arange(number_of)

    def named(sizes, offset_by):
        used = int((sizes > 0).sum())
        fixed = max(1, used // 4)
        moved = fixed + (places - fixed + offset_by * (used - fixed)) % max(1, number_of - fixed)
        return jnp.zeros((number_of,), jnp.int32).at[order[jnp.where(places < fixed, places, moved)]].set(jnp.asarray(sizes, jnp.int32))

    sizes = jnp.where(number % 4 == 0, named(packed, number // 4), named(usual, number - number // 4 - 1))
    mixed = jax.random.permutation(jax.random.fold_in(own, 3), number_of)
    source_of, receiver = mixed[0:number_of // 2 * 2:2], mixed[1:number_of // 2 * 2:2]
    room = jnp.minimum(sizes[source_of] - 1, reach - sizes[receiver]) // 2
    room = jnp.where((source_of == order[0]) | (receiver == order[0]) | (sizes[receiver] == 0), 0, jnp.maximum(room, 0))
    moved = jax.random.randint(jax.random.fold_in(own, 4), (number_of // 2,), 0, 1 << 20) % (room + 1)
    sizes = sizes.at[source_of].add(-moved).at[receiver].add(moved)
    labels = jnp.searchsorted(jnp.cumsum(sizes), jnp.arange(rows * top), side="right").astype(jnp.int32)
    table = labels.reshape(top, rows).T
    table = table[jax.random.permutation(jax.random.fold_in(own, 1), rows)]
    offset_by = jax.random.randint(jax.random.fold_in(own, 2), (rows, 1), 0, top)
    return jnp.take_along_axis(table, (jnp.arange(top)[None, :] + offset_by) % top, axis=1)


def portions_of(number_of, total, bound, lean, full):
    portions = [(1 << 20) // math.isqrt(rank ** lean) + 1 for rank in range(1, number_of + 1)]
    largest = bound if full else min(bound, max(-(-total // number_of), total * portions[0] // sum(portions)))
    least = 1 if total - largest >= number_of - 1 else 0
    counts, surplus = [largest] + [least] * (number_of - 1), total - largest - least * (number_of - 1)
    while surplus > 0:
        movable = [i for i in range(1, number_of) if counts[i] < largest] or [i for i in range(1, number_of) if counts[i] < bound]
        mass, left = sum([portions[i] for i in movable]), surplus
        for i in movable:
            more = min(bound - counts[i], max(1, left * portions[i] // mass), surplus)
            counts[i] = counts[i] + more
            surplus = surplus - more
    return np.array(counts)


def gaussian(own_key, shape, deviation, reach, cuts=(), kind=jnp.bfloat16):
    level = level_of(own_key, shape, cuts, -0.22, 0.18) if cuts else 1.0
    values = jax.random.normal(own_key, shape, jnp.float32) * deviation * level
    return jnp.minimum(jnp.maximum(values, -reach), reach).astype(kind)


def setup_inputs(seed: int = 0) -> dict:
    splits = jax.random.split(jax.random.key(seed), 9)
    decoder_input = draw_decoder_input(jax.random.fold_in(splits[8], 71), 0)
    reward_grad = gaussian(splits[1], (CLIPS, REWARD_SLOTS, ROWS, CHANNELS, WIDTH), 1.0, 6.0, ((0, 16), (1, 16)))
    reward_owner_keys = jax.random.split(jax.random.fold_in(splits[2], 1), CLIPS * FRAMES // FRAMES)
    reward_owner_turns = jax.random.permutation(jax.random.fold_in(splits[2], 3), CLIPS * FRAMES // FRAMES)
    reward_owner = jax.vmap(lambda own, number: shared_out(jax.random.fold_in(splits[2], 2), own, number, FRAMES, N_TILE, 1, SLOTS, 2))(reward_owner_keys, reward_owner_turns).reshape((CLIPS, FRAMES, 1))
    scored_frame = plant(jax.random.randint(splits[3], (CLIPS, FRAMES), 0, FRAMES), jax.random.fold_in(splits[3], 1), 0, FRAMES - 1).astype(jnp.int32)
    first_gain = jnp.clip(1.0 + 0.18 * jax.random.normal(splits[4], (CHANNELS,), jnp.float32), 0.1, 1.9)
    second_gain = jnp.clip(1.0 + 0.18 * jax.random.normal(splits[5], (CHANNELS,), jnp.float32), 0.1, 1.9)
    first_kernel = gaussian(splits[6], (3, 3, 3, CHANNELS, CHANNELS), (27 * CHANNELS) ** -0.5, 0.125)
    second_kernel = gaussian(splits[7], (3, 3, 3, CHANNELS, CHANNELS), (27 * CHANNELS) ** -0.5, 0.125)
    return dict(decoder_input=decoder_input, reward_grad=reward_grad, reward_owner=reward_owner, scored_frame=scored_frame, first_gain=first_gain, second_gain=second_gain, first_kernel=first_kernel, second_kernel=second_kernel)


epsilon = 1e-06
highest = lax.Precision.HIGHEST

def slot_table(owners, scored, device_count, slot_count, frames):
    onehot = (owners[:, None] == jnp.arange(device_count, dtype=jnp.int32)[None, :]).astype(jnp.int32)
    before = jnp.cumsum(onehot, axis=0) - onehot
    ranking = lax.optimization_barrier(jnp.sum(before * onehot, axis=1))
    position = owners * slot_count + ranking
    by_frame = (scored[None, :] == jnp.arange(frames, dtype=jnp.int32)[:, None]).astype(jnp.float32)
    by_slot = (position[:, None] == jnp.arange(device_count * slot_count, dtype=jnp.int32)[None, :]).astype(jnp.float32)
    return jnp.dot(by_frame, by_slot, preferred_element_type=jnp.float32)

def pad_rows(values):
    return jnp.pad(values, ((0, 0), (1, 1), (0, 0), (0, 0)))

def conv_forward(padded_rows, kernel):
    frames = padded_rows.shape[0]
    row_count = padded_rows.shape[1] - 2
    col_count = padded_rows.shape[3]
    padded = jnp.pad(padded_rows.astype(jnp.float32), ((2, 0), (0, 0), (0, 0), (1, 1)))
    weights = kernel.astype(jnp.float32)
    summed = jnp.zeros((frames, row_count, weights.shape[3], col_count), jnp.float32)
    for time_tap in range(3):
        for row_tap in range(3):
            stacked = jnp.stack([padded[time_tap:time_tap + frames, row_tap:row_tap + row_count, :, col_tap:col_tap + col_count] for col_tap in range(3)], axis=2)
            summed = summed + jnp.einsum('koi,fhkiw->fhow', weights[time_tap, row_tap], stacked, precision=highest)
    return summed

def conv_input_grad(padded_rows, kernel):
    frames = padded_rows.shape[0]
    row_count = padded_rows.shape[1] - 2
    col_count = padded_rows.shape[3]
    padded = jnp.pad(padded_rows.astype(jnp.float32), ((0, 2), (0, 0), (0, 0), (1, 1)))
    weights = kernel.astype(jnp.float32)
    summed = jnp.zeros((frames, row_count, weights.shape[4], col_count), jnp.float32)
    for time_tap in range(3):
        for row_tap in range(3):
            stacked = jnp.stack([padded[2 - time_tap:2 - time_tap + frames, 2 - row_tap:2 - row_tap + row_count, :, 2 - col_tap:2 - col_tap + col_count] for col_tap in range(3)], axis=2)
            summed = summed + jnp.einsum('koi,fhkow->fhiw', weights[time_tap, row_tap], stacked, precision=highest)
    return summed

def conv_weight_grad(padded_rows, grad_out):
    frames = grad_out.shape[0]
    row_count = grad_out.shape[1]
    col_count = grad_out.shape[3]
    padded = jnp.pad(padded_rows.astype(jnp.float32), ((2, 0), (0, 0), (0, 0), (1, 1)))
    grad_float = grad_out.astype(jnp.float32)
    pieces = []
    for time_tap in range(3):
        for row_tap in range(3):
            stacked = jnp.stack([padded[time_tap:time_tap + frames, row_tap:row_tap + row_count, :, col_tap:col_tap + col_count] for col_tap in range(3)], axis=2)
            pieces.append(jnp.einsum('fhow,fhkiw->koi', grad_float, stacked, precision=highest))
    return jnp.stack(pieces).reshape(3, 3, 3, grad_out.shape[2], padded_rows.shape[2])

def norm_inverse(values):
    return lax.rsqrt(lax.optimization_barrier(jnp.mean(values * values, axis=2, keepdims=True)) + epsilon)

def norm_backward(grad_act, normed, inverse, norm_gain):
    gained = normed * norm_gain[None, None, :, None]
    sigmoid_unit = jax.nn.sigmoid(gained)
    scaled = grad_act.astype(jnp.float32) * sigmoid_unit * (1.0 + gained * (1.0 - sigmoid_unit)) * norm_gain[None, None, :, None]
    mean_two = lax.optimization_barrier(jnp.mean(scaled * normed, axis=2, keepdims=True))
    return inverse * (scaled - normed * mean_two)

def reference(decoder_input, reward_grad, reward_owner, scored_frame, first_gain, second_gain, first_kernel, second_kernel):

    def per_clip(totals, clip_inputs):
        features, reward_rows, owners, scored = clip_inputs
        slot_map = slot_table(owners[:, 0], scored, N_TILE, SLOTS, FRAMES)
        grad_out = jnp.einsum('fs,shcw->fhcw', slot_map, reward_rows.astype(jnp.float32), precision=highest).astype(jnp.bfloat16)
        inputs_float = features.astype(jnp.float32)
        inverse_in = norm_inverse(inputs_float)
        normed_in = inputs_float * inverse_in
        act_in = jax.nn.silu(normed_in * first_gain[None, None, :, None]).astype(jnp.bfloat16)
        act_in_rows = pad_rows(act_in)
        hidden = conv_forward(act_in_rows, first_kernel).astype(jnp.bfloat16)
        hidden_float = hidden.astype(jnp.float32)
        inverse_mid = norm_inverse(hidden_float)
        normed_mid = hidden_float * inverse_mid
        act_mid = jax.nn.silu(normed_mid * second_gain[None, None, :, None]).astype(jnp.bfloat16)
        second_local = conv_weight_grad(pad_rows(act_mid), grad_out)
        grad_mid = conv_input_grad(pad_rows(grad_out), second_kernel).astype(jnp.bfloat16)
        grad_hidden = norm_backward(grad_mid, normed_mid, inverse_mid, second_gain).astype(jnp.bfloat16)
        first_local = conv_weight_grad(act_in_rows, grad_hidden)
        grad_in = conv_input_grad(pad_rows(grad_hidden), first_kernel).astype(jnp.bfloat16)
        feature_grad = (grad_out.astype(jnp.float32) + norm_backward(grad_in, normed_in, inverse_in, first_gain)).astype(jnp.bfloat16)
        return ((totals[0] + first_local, totals[1] + second_local), feature_grad)
    empty = jnp.zeros((3, 3, 3, CHANNELS, CHANNELS), jnp.float32)
    totals, feature_grad = lax.scan(per_clip, (empty, empty), (decoder_input, reward_grad, reward_owner, scored_frame))
    grad_scale = 1.0 / math.sqrt(CLIPS * FRAMES * ROWS * WIDTH)
    return (feature_grad, totals[0] * grad_scale, totals[1] * grad_scale)
```

```python
import functools

import jax
import jax.numpy as jnp
from jax import lax
from jax.experimental import pallas as pl
from jax.experimental.pallas import tpu as pltpu
from jax.sharding import PartitionSpec as P

MESH = pl.DeviceIdType.MESH
F32 = jnp.float32
BF16 = jnp.bfloat16
epsilon = 1e-06

FRAMES = 16
TILES = 16
CLIPS = 16
C = 96
W = 128
TAPS = 9 * C
PADDED = 896
UNROLL = 2


def inverse_rms(x):
    return lax.rsqrt(jnp.mean(x * x, axis=0, keepdims=True) + epsilon)


def sigmoid(u):
    return 0.5 * jnp.tanh(0.5 * u) + 0.5


def norm_silu(x, gain):
    u = gain * (x * inverse_rms(x))
    return u * sigmoid(u)


def norm_backward(g, x, gain):
    r = inverse_rms(x)
    normed = x * r
    u = gain * normed
    sig = sigmoid(u)
    q = g * gain * sig * (1.0 + u * (1.0 - sig))
    p = jnp.mean(q * normed, axis=0, keepdims=True)
    return r * (q - normed * p)


def put_row(y_ref, f, r, value):
    lane = lax.broadcasted_iota(jnp.int32, (C, W), 1)
    wide = value.astype(F32)
    low = jnp.where(lane == 0, 0.0, pltpu.roll(wide, 1, 1)).astype(BF16)
    high = jnp.where(lane == W - 1, 0.0, pltpu.roll(wide, W - 1, 1)).astype(BF16)
    for e, v in enumerate((low, value, high)):
        for b in range(3):
            h = r - b
            if 0 <= h < 2:
                y_ref[f, (b * 3 + e) * C:(b * 3 + e + 1) * C, h * W:(h + 1) * W] = v


def kernel(
    x_ref, rw_ref, own_col_ref, own_row_ref, scored_ref, g1_ref, g2_ref, k1_ref, k2_ref,
    out_ref, res_ref,
    rin, rrw, k1f, k1t, k2t, g1c, g2c, pick,
    x4, xg4, xh4, yin, yg, yh, hid, act, gh, c1, c2, fb,
    w1, w2, bb, r0, r1, cc, r2,
    in_s, in_r, rw_s, rw_r, loc, halo_s, halo_r, f_s, f_r,
    s0_s, s0_r, s1_s, s1_r, s2_s, s2_r, a2_s, a2_r, a1_s, a1_r, a0_s, a0_r,
):
    clip = lax.axis_index("clip")
    me = lax.axis_index("tile")
    core = me % 2
    z = me // 2
    sibling = me + 1 - 2 * core

    def tile_peer(i):
        step = i // 2 + 1
        return (me + (1 - i % 2) * step + (i % 2) * (TILES - step)) % TILES

    def clip_peer(i):
        return (clip + i + 1) % CLIPS

    def z_peer(i):
        return ((z + i + 1) % 8) * 2 + core

    def loop(n, body):
        def step(i, carry):
            body(i)
            return carry

        lax.fori_loop(0, n, step, 0)

    barrier = pltpu.get_barrier_semaphore()
    loop(15, lambda i: pl.semaphore_signal(
        barrier, inc=1, device_id=(clip, tile_peer(i)), device_id_type=MESH))
    loop(15, lambda i: pl.semaphore_signal(
        barrier, inc=1, device_id=(clip_peer(i), me), device_id_type=MESH))
    pl.semaphore_wait(barrier, 30)

    def in_copy(src, dst, slot, peer):
        return pltpu.make_async_remote_copy(
            src_ref=x_ref.at[pl.ds(2 * src, 2)], dst_ref=rin.at[dst],
            send_sem=in_s.at[src], recv_sem=in_r.at[slot],
            device_id=(clip, peer), device_id_type=MESH)

    def rw_copy(src, dst, slot, peer):
        return pltpu.make_async_remote_copy(
            src_ref=rw_ref.at[:, pl.ds(2 * src, 2)], dst_ref=rrw.at[dst],
            send_sem=rw_s.at[src], recv_sem=rw_r.at[slot],
            device_id=(clip, peer), device_id_type=MESH)

    own_in = pltpu.make_async_copy(x_ref.at[pl.ds(2 * me, 2)], rin.at[me], loc.at[0])
    own_rw = pltpu.make_async_copy(rw_ref.at[:, pl.ds(2 * me, 2)], rrw.at[me], loc.at[1])

    def start_in(i):
        peer = tile_peer(14 - i)
        in_copy(peer, me, me, peer).start()

    def start_rw(i):
        peer = tile_peer(14 - i)
        rw_copy(peer, me, me, peer).start()

    loop(15, start_in)
    own_in.start()
    loop(15, start_rw)
    own_rw.start()

    def column(row_ref):
        row = lax.broadcasted_iota(jnp.int32, (C, C), 0)
        col = lax.broadcasted_iota(jnp.int32, (C, C), 1)
        wide = jnp.broadcast_to(row_ref[...], (C, C))
        return jnp.broadcast_to(
            jnp.sum(jnp.where(row == col, wide, 0.0), axis=1, keepdims=True), (C, W))

    g1c[...] = column(g1_ref)
    g2c[...] = column(g2_ref)

    own_col, own_row = own_col_ref[...], own_row_ref[...]
    earlier = (lax.broadcasted_iota(jnp.int32, (16, 16), 1)
               < lax.broadcasted_iota(jnp.int32, (16, 16), 0))
    same = own_col == own_row
    ranking = jnp.sum(jnp.where(same & earlier, 1, 0), axis=1, keepdims=True)
    slot = own_col * 2 + ranking
    by_slot = jnp.where(
        slot == lax.shift_right_logical(lax.broadcasted_iota(jnp.int32, (16, 512), 1), 4),
        1.0, 0.0)
    by_frame = jnp.where(
        scored_ref[...]
        == lax.shift_right_logical(lax.broadcasted_iota(jnp.int32, (256, 16), 0), 4),
        1.0, 0.0)
    table = jnp.dot(by_frame, by_slot, preferred_element_type=F32)
    row16 = lax.broadcasted_iota(jnp.int32, (256, 512), 0) & 15
    col16 = lax.broadcasted_iota(jnp.int32, (256, 512), 1) & 15
    pick[...] = jnp.where(row16 == col16, table, 0.0).astype(BF16)

    for a in range(3):
        rows = slice(a * C, (a + 1) * C)
        k1f[rows, :] = jnp.concatenate(
            [k1_ref[a * 9 + i].astype(F32) for i in range(9)], axis=1).astype(BF16)
        k1t[rows, :] = jnp.transpose(jnp.concatenate(
            [k1_ref[a * 9 + 8 - i] for i in range(9)], axis=0).astype(F32)).astype(BF16)
        k2t[rows, :] = jnp.transpose(jnp.concatenate(
            [k2_ref[a * 9 + 8 - i] for i in range(9)], axis=0).astype(F32)).astype(BF16)

    act[0:2] = jnp.zeros((2, C, 2 * W), BF16)
    gh[16:18] = jnp.zeros((2, C, 2 * W), BF16)
    w1[...] = jnp.zeros_like(w1)
    w2[...] = jnp.zeros_like(w2)
    bb[252:256] = jnp.zeros((4, 2, 8, 128), F32)

    low_peer, high_peer = (me + TILES - 1) % TILES, (me + 1) % TILES

    def halo_pair(ref, k):
        up = pltpu.make_async_remote_copy(
            src_ref=ref.at[2], dst_ref=ref.at[0],
            send_sem=halo_s.at[2 * k], recv_sem=halo_r.at[2 * k],
            device_id=(clip, high_peer), device_id_type=MESH)
        down = pltpu.make_async_remote_copy(
            src_ref=ref.at[1], dst_ref=ref.at[3],
            send_sem=halo_s.at[2 * k + 1], recv_sem=halo_r.at[2 * k + 1],
            device_id=(clip, low_peer), device_id_type=MESH)
        return up, down

    def put_halo(ref, y_ref):
        def body(f):
            put_row(y_ref, f, 0, jnp.where(me > 0, ref[0, f].astype(F32), 0.0).astype(BF16))
            put_row(y_ref, f, 3, jnp.where(me < TILES - 1, ref[3, f].astype(F32), 0.0).astype(BF16))

        loop(FRAMES, body)

    def first(f):
        for h in range(2):
            v = norm_silu(rin[f, h].astype(F32), g1c[...]).astype(BF16)
            x4[1 + h, f] = v
            put_row(yin, f, 1 + h, v)

    own_in.wait()
    first(me)

    def arrived(i):
        src = tile_peer(i)
        in_copy(src, src, src, src).wait_recv()
        first(src)

    loop(15, arrived)
    halo = halo_pair(x4, 0)
    for copy in halo:
        copy.start()
    for copy in halo:
        copy.wait()
    put_halo(x4, yin)

    def conv(kernel_ref, y_ref, reverse, each):
        c1[...] = jnp.zeros_like(c1)
        c2[...] = jnp.zeros_like(c2)

        def body(i):
            one, two = c1[...], c2[...]
            for k in range(UNROLL):
                f = i * UNROLL + k
                if reverse:
                    f = FRAMES - 1 - f
                p = jnp.dot(kernel_ref[...], y_ref[f], preferred_element_type=F32)
                each(f, (p[2 * C:] + one).astype(BF16))
                one = p[C:2 * C] + two
                two = p[:C]
            c1[...] = one
            c2[...] = two

        loop(FRAMES // UNROLL, body)

    def mid(f, h):
        hid[f] = h
        for row in range(2):
            lanes = slice(row * W, (row + 1) * W)
            act[f + 2, :, lanes] = norm_silu(h[:, lanes].astype(F32), g2c[...]).astype(BF16)

    conv(k1f, yin, False, mid)

    def rw_arrived(i):
        src = tile_peer(i)
        rw_copy(src, src, src, src).wait_recv()

    own_rw.wait()
    loop(15, rw_arrived)
    for i in range(C // 16):
        rows = slice(16 * i, 16 * i + 16)
        slots = jnp.concatenate(
            [rrw[:, :, h, rows, :].reshape(512, W) for h in range(2)], axis=1)
        og = jnp.dot(pick[...], slots, preferred_element_type=F32).astype(BF16)
        og = og.reshape(FRAMES, 16, 2 * W)
        xg4[1, :, rows, :] = og[:, :, :W]
        xg4[2, :, rows, :] = og[:, :, W:]
    halo = halo_pair(xg4, 1)
    for copy in halo:
        copy.start()

    def put_own(ref, y_ref):
        def body(f):
            for h in range(2):
                put_row(y_ref, f, 1 + h, ref[1 + h, f])

        loop(FRAMES, body)

    put_own(xg4, yg)
    for copy in halo:
        copy.wait()
    put_halo(xg4, yg)

    def back_mid(f, g):
        for row in range(2):
            lanes = slice(row * W, (row + 1) * W)
            v = norm_backward(
                g[:, lanes].astype(F32), hid[f, :, lanes].astype(F32), g2c[...]).astype(BF16)
            xh4[1 + row, f] = v
            gh[f, :, lanes] = v
            put_row(yh, f, 1 + row, v)

    conv(k2t, yg, True, back_mid)
    halo = halo_pair(xh4, 2)
    for copy in halo:
        copy.start()

    def weight(left, y_ref, w_ref):
        def body(i):
            total = w_ref[:, :TAPS]
            for k in range(4):
                f = i * 4 + k
                total = total + lax.dot_general(
                    left(f), y_ref[f], (((1,), (1,)), ((), ())), preferred_element_type=F32)
            w_ref[:, :TAPS] = total

        loop(FRAMES // 4, body)

    weight(lambda f: jnp.concatenate([gh[f + 2], gh[f + 1], gh[f]], axis=0), yin, w1)
    weight(lambda f: act[pl.ds(f, 3)].reshape(3 * C, 2 * W), yg, w2)

    def pack(i):
        for n, w_ref in enumerate((w1, w2)):
            rows = w_ref[pl.ds(pl.multiple_of(8 * i, 8), 8), :]
            for j in range(7):
                bb[7 * i + j, n] = rows[:, 128 * j:128 * (j + 1)]

    loop(36, pack)
    mine, other = core * 128, (1 - core) * 128
    s0 = pltpu.make_async_remote_copy(
        src_ref=bb.at[pl.ds(other, 128)], dst_ref=r0, send_sem=s0_s.at[0], recv_sem=s0_r.at[0],
        device_id=(clip, sibling), device_id_type=MESH)
    s0.start()

    for copy in halo:
        copy.wait()
    put_halo(xh4, yh)

    s0.wait()

    def add0(i):
        at = pl.ds(mine + 8 * i, 8)
        bb[at] = bb[at] + r0[pl.ds(8 * i, 8)]

    loop(16, add0)

    def s1_copy(piece, slot_at, peer):
        return pltpu.make_async_remote_copy(
            src_ref=bb.at[pl.ds(mine + 8 * piece, 8)], dst_ref=r1.at[slot_at],
            send_sem=s1_s.at[piece], recv_sem=s1_r.at[slot_at],
            device_id=(peer, me), device_id_type=MESH)

    loop(15, lambda i: s1_copy(clip_peer(i), clip, clip_peer(i)).start())

    def f_copy(f, dst_rows, slot_at, peer):
        return pltpu.make_async_remote_copy(
            src_ref=fb.at[f], dst_ref=out_ref.at[pl.ds(2 * dst_rows, 2)],
            send_sem=f_s.at[f], recv_sem=f_r.at[slot_at],
            device_id=(clip, peer), device_id_type=MESH)

    own_out = pltpu.make_async_copy(fb.at[me], out_ref.at[pl.ds(2 * me, 2)], loc.at[2])

    def back_in(f, g):
        for row in range(2):
            v = norm_backward(
                g[:, row * W:(row + 1) * W].astype(F32), rin[f, row].astype(F32), g1c[...])
            fb[f, row] = (xg4[1 + row, f].astype(F32) + v).astype(BF16)

        @pl.when(f != me)
        def _():
            f_copy(f, me, me, f).start()

        @pl.when(f == me)
        def _():
            own_out.start()

    conv(k1t, yh, True, back_in)

    loop(15, lambda i: s1_copy(clip_peer(i), clip_peer(i), clip_peer(i)).wait())
    r1[clip] = bb[pl.ds(mine + 8 * clip, 8)]

    def add1(i):
        total = r1[0, i]
        for p in range(1, CLIPS):
            total = total + r1[p, i]
        cc[i] = total

    loop(8, add1)

    def s2_copy(zz, slot_at, peer):
        return pltpu.make_async_remote_copy(
            src_ref=cc.at[zz], dst_ref=r2.at[slot_at],
            send_sem=s2_s.at[zz], recv_sem=s2_r.at[slot_at],
            device_id=(clip, peer), device_id_type=MESH)

    def z_of(i):
        return (z + i + 1) % 8

    loop(7, lambda i: s2_copy(z_of(i), z, z_peer(i)).start())
    r2[z] = cc[z]
    loop(7, lambda i: s2_copy(z_of(i), z_of(i), z_peer(i)).wait())
    total = r2[0]
    for p in range(1, 8):
        total = total + r2[p]
    base = mine + 8 * clip
    res_ref[base + z] = total

    def a2_copy(at, sem_at, peer):
        return pltpu.make_async_remote_copy(
            src_ref=res_ref.at[base + at], dst_ref=res_ref.at[base + at],
            send_sem=a2_s.at[sem_at], recv_sem=a2_r.at[at],
            device_id=(clip, peer), device_id_type=MESH)

    loop(7, lambda i: a2_copy(z, z_of(i), z_peer(i)).start())

    def a2_wait(i):
        a2_copy(z_of(i), z_of(i), z_peer(i)).wait_recv()
        a2_copy(z, z_of(i), z_peer(i)).wait_send()

    loop(7, a2_wait)

    def a1_copy(at, sem_at, peer):
        piece = res_ref.at[pl.ds(mine + 8 * at, 8)]
        return pltpu.make_async_remote_copy(
            src_ref=piece, dst_ref=piece, send_sem=a1_s.at[sem_at], recv_sem=a1_r.at[at],
            device_id=(peer, me), device_id_type=MESH)

    loop(15, lambda i: a1_copy(clip, clip_peer(i), clip_peer(i)).start())

    def a1_wait(i):
        a1_copy(clip_peer(i), clip_peer(i), clip_peer(i)).wait_recv()
        a1_copy(clip, clip_peer(i), clip_peer(i)).wait_send()

    loop(15, a1_wait)

    def a0_copy(half):
        piece = res_ref.at[pl.ds(half, 128)]
        return pltpu.make_async_remote_copy(
            src_ref=piece, dst_ref=piece, send_sem=a0_s.at[0], recv_sem=a0_r.at[0],
            device_id=(clip, sibling), device_id_type=MESH)

    a0_copy(mine).start()
    a0_copy(other).wait_recv()
    a0_copy(mine).wait_send()

    own_out.wait()

    def drain(i):
        peer = tile_peer(i)
        f_copy(peer, peer, peer, peer).wait_recv()
        f_copy(peer, me, me, peer).wait_send()
        in_copy(peer, me, me, peer).wait_send()
        rw_copy(peer, me, me, peer).wait_send()

    loop(15, drain)


def unpack(scale, p_ref, o1_ref, o2_ref, s_ref):
    for n, o_ref in enumerate((o1_ref, o2_ref)):
        def body(i, carry):
            for j in range(7):
                s_ref[pl.ds(pl.multiple_of(8 * i, 8), 8), 128 * j:128 * (j + 1)] = (
                    p_ref[7 * i + j, n] * scale)
            return carry

        lax.fori_loop(0, 36, body, 0)
        for a in range(3):
            for i in range(9):
                block = s_ref[a * C:(a + 1) * C, i * C:(i + 1) * C]
                if n == 0:
                    o_ref[a * 9 + i] = block
                else:
                    o_ref[a * 9 + 8 - i] = jnp.transpose(block)


def local(
    decoder_input, reward_grad, reward_owner, scored_frame,
    first_gain, second_gain, first_kernel, second_kernel,
):
    vmem = pl.BlockSpec(memory_space=pltpu.VMEM)
    hbm = pl.BlockSpec(memory_space=pl.ANY)
    dma = pltpu.SemaphoreType.DMA
    feature, packed = pl.pallas_call(
        kernel,
        out_shape=(
            jax.ShapeDtypeStruct((32, C, W), BF16),
            jax.ShapeDtypeStruct((256, 2, 8, 128), F32),
        ),
        in_specs=[hbm, hbm] + [vmem] * 7,
        out_specs=(hbm, vmem),
        scratch_shapes=[
            pltpu.VMEM((16, 2, C, W), BF16),
            pltpu.VMEM((16, 2, 2, C, W), BF16),
            pltpu.VMEM((3 * C, TAPS), BF16),
            pltpu.VMEM((3 * C, TAPS), BF16),
            pltpu.VMEM((3 * C, TAPS), BF16),
            pltpu.VMEM((C, W), F32),
            pltpu.VMEM((C, W), F32),
            pltpu.VMEM((256, 512), BF16),
            pltpu.VMEM((4, 16, C, W), BF16),
            pltpu.VMEM((4, 16, C, W), BF16),
            pltpu.VMEM((4, 16, C, W), BF16),
            pltpu.VMEM((16, TAPS, 2 * W), BF16),
            pltpu.VMEM((16, TAPS, 2 * W), BF16),
            pltpu.VMEM((16, TAPS, 2 * W), BF16),
            pltpu.VMEM((16, C, 2 * W), BF16),
            pltpu.VMEM((18, C, 2 * W), BF16),
            pltpu.VMEM((18, C, 2 * W), BF16),
            pltpu.VMEM((C, 2 * W), F32),
            pltpu.VMEM((C, 2 * W), F32),
            pltpu.VMEM((16, 2, C, W), BF16),
            pltpu.VMEM((3 * C, PADDED), F32),
            pltpu.VMEM((3 * C, PADDED), F32),
            pltpu.VMEM((256, 2, 8, 128), F32),
            pltpu.VMEM((128, 2, 8, 128), F32),
            pltpu.VMEM((16, 8, 2, 8, 128), F32),
            pltpu.VMEM((8, 2, 8, 128), F32),
            pltpu.VMEM((8, 2, 8, 128), F32),
            dma((16,)), dma((16,)), dma((16,)), dma((16,)), dma((3,)),
            dma((6,)), dma((6,)), dma((16,)), dma((16,)),
            dma((1,)), dma((1,)), dma((16,)), dma((16,)), dma((8,)), dma((8,)),
            dma((8,)), dma((8,)), dma((16,)), dma((16,)), dma((1,)), dma((1,)),
        ],
        compiler_params=pltpu.CompilerParams(
            collective_id=0, has_side_effects=True, vmem_limit_bytes=56 * 2**20),
    )(
        decoder_input[0, 0],
        reward_grad[0],
        reward_owner[0],
        reward_owner[0].reshape(1, 16),
        scored_frame,
        first_gain.reshape(1, C),
        second_gain.reshape(1, C),
        first_kernel.reshape(27, C, C),
        second_kernel.reshape(27, C, C),
    )
    first_total, second_total = pl.pallas_call(
        functools.partial(unpack, 1.0 / 1024.0),
        out_shape=(jax.ShapeDtypeStruct((27, C, C), F32),) * 2,
        in_specs=[vmem],
        out_specs=(vmem, vmem),
        scratch_shapes=[pltpu.VMEM((3 * C, PADDED), F32)],
        compiler_params=pltpu.CompilerParams(vmem_limit_bytes=32 * 2**20),
    )(packed)
    shape = (3, 3, 3, C, C)
    return feature[None, None], first_total.reshape(shape), second_total.reshape(shape)


def solution(mesh):
    in_specs = (
        P("clip", "tile", None, None, None),
        P("clip", "tile", None, None, None),
        P("clip", None, None),
        P("clip", None),
        P(),
        P(),
        P(),
        P(),
    )
    out_specs = (P("clip", "tile", None, None, None), P(), P())
    return jax.shard_map(local, mesh=mesh, in_specs=in_specs, out_specs=out_specs, check_vma=False)
```

```python
import functools

import jax
import jax.numpy as jnp
from jax import lax
from jax.experimental import pallas as pl
from jax.experimental.pallas import tpu as pltpu
from jax.sharding import PartitionSpec as P

MESH = pl.DeviceIdType.MESH
F32 = jnp.float32
BF16 = jnp.bfloat16
epsilon = 1e-06

FRAMES = 16
TILES = 16
CLIPS = 16
C = 96
W = 128
TAPS = 9 * C
PADDED = 896
UNROLL = 2
EARLY = 4


def inverse_rms(x):
    return lax.rsqrt(jnp.mean(x * x, axis=0, keepdims=True) + epsilon)


def sigmoid(u):
    return 0.5 * jnp.tanh(0.5 * u) + 0.5


def norm_silu(x, gain):
    u = gain * (x * inverse_rms(x))
    return u * sigmoid(u)


def norm_backward(g, x, gain):
    r = inverse_rms(x)
    normed = x * r
    u = gain * normed
    sig = sigmoid(u)
    q = g * gain * sig * (1.0 + u * (1.0 - sig))
    p = jnp.mean(q * normed, axis=0, keepdims=True)
    return r * (q - normed * p)


def mid_both(g, x, gain):
    r = inverse_rms(x)
    normed = x * r
    u = gain * normed
    sig = sigmoid(u)
    q = g * gain * sig * (1.0 + u * (1.0 - sig))
    p = jnp.mean(q * normed, axis=0, keepdims=True)
    return u * sig, r * (q - normed * p)


def put_row(y_ref, f, r, value):
    lane = lax.broadcasted_iota(jnp.int32, (C, W), 1)
    wide = value.astype(F32)
    low = jnp.where(lane == 0, 0.0, pltpu.roll(wide, 1, 1)).astype(BF16)
    high = jnp.where(lane == W - 1, 0.0, pltpu.roll(wide, W - 1, 1)).astype(BF16)
    for e, v in enumerate((low, value, high)):
        for b in range(3):
            h = r - b
            if 0 <= h < 2:
                y_ref[f, (b * 3 + e) * C:(b * 3 + e + 1) * C, h * W:(h + 1) * W] = v


def kernel(
    x_ref, rw_ref, own_ref, scored_ref, g1_ref, g2_ref, k1_ref, k2_ref,
    out_ref, res_ref,
    rin, rrw, k1f, k1t, k2t, g1c, g2c, pick,
    x4, xg4, xh4, yin, yg, yh, gm, act, gh, c1, c2, fb,
    w, bb, sb, r0, s1b, r1, c16, r2,
    in_s, in_r, rw_s, rw_r, loc, halo_s, halo_r, f_s, f_r,
    s0_s, s0_r, s1_s, s1_r, s2_s, s2_r, a1_s, a1_r, a0_s, a0_r,
):
    clip = lax.axis_index("clip")
    me = lax.axis_index("tile")
    core = me % 2
    z = me // 2
    sibling = me + 1 - 2 * core

    def tile_peer(i):
        step = i // 2 + 1
        return (me + (1 - i % 2) * step + (i % 2) * (TILES - step)) % TILES

    def clip_peer(i):
        return (clip + i + 1) % CLIPS

    def z_of(i):
        return (z + i + 1) % 8

    def loop(n, body):
        def step(i, carry):
            body(i)
            return carry

        lax.fori_loop(0, n, step, 0)

    barrier = pltpu.get_barrier_semaphore()
    loop(15, lambda i: pl.semaphore_signal(
        barrier, inc=1, device_id=(clip, tile_peer(i)), device_id_type=MESH))
    loop(15, lambda i: pl.semaphore_signal(
        barrier, inc=1, device_id=(clip_peer(i), me), device_id_type=MESH))

    def column(row, n, zero):
        eye = (lax.broadcasted_iota(jnp.int32, (n, n), 0)
               == lax.broadcasted_iota(jnp.int32, (n, n), 1))
        return jnp.sum(jnp.where(eye, jnp.broadcast_to(row, (n, n)), zero), axis=1, keepdims=True)

    g1c[...] = jnp.broadcast_to(column(g1_ref[...], C, 0.0), (C, W))
    g2c[...] = jnp.broadcast_to(column(g2_ref[...], C, 0.0), (C, W))

    own_row = own_ref[...]
    own_col = column(own_row, 16, 0)
    earlier = (lax.broadcasted_iota(jnp.int32, (16, 16), 1)
               < lax.broadcasted_iota(jnp.int32, (16, 16), 0))
    same = own_col == own_row
    ranking = jnp.sum(jnp.where(same & earlier, 1, 0), axis=1, keepdims=True)
    slot = own_col * 2 + ranking
    by_slot = jnp.where(
        slot == lax.shift_right_logical(lax.broadcasted_iota(jnp.int32, (16, 512), 1), 4),
        1.0, 0.0)
    by_frame = jnp.where(
        scored_ref[...]
        == lax.shift_right_logical(lax.broadcasted_iota(jnp.int32, (256, 16), 0), 4),
        1.0, 0.0)
    table = jnp.dot(by_frame, by_slot, preferred_element_type=F32)
    row16 = lax.broadcasted_iota(jnp.int32, (256, 512), 0) & 15
    col16 = lax.broadcasted_iota(jnp.int32, (256, 512), 1) & 15
    pick[...] = jnp.where(row16 == col16, table, 0.0).astype(BF16)

    for a in range(3):
        rows = slice(a * C, (a + 1) * C)
        k1f[rows, :] = jnp.concatenate(
            [k1_ref[a * 9 + i].astype(F32) for i in range(9)], axis=1).astype(BF16)
        k1t[rows, :] = jnp.transpose(jnp.concatenate(
            [k1_ref[a * 9 + 8 - i] for i in range(9)], axis=0).astype(F32)).astype(BF16)
        k2t[rows, :] = jnp.transpose(jnp.concatenate(
            [k2_ref[a * 9 + 8 - i] for i in range(9)], axis=0).astype(F32)).astype(BF16)

    act[0:2] = jnp.zeros((2, C, 2 * W), BF16)
    gh[16:18] = jnp.zeros((2, C, 2 * W), BF16)
    w[...] = jnp.zeros_like(w)
    for n in range(2):
        bb[n, 126:128] = jnp.zeros((2, 16, 128), F32)
        sb[n, 126:128] = jnp.zeros((2, 16, 128), BF16)

    pl.semaphore_wait(barrier, 30)

    def in_copy(src, dst, slot, peer):
        return pltpu.make_async_remote_copy(
            src_ref=x_ref.at[pl.ds(2 * src, 2)], dst_ref=rin.at[dst],
            send_sem=in_s.at[src], recv_sem=in_r.at[slot],
            device_id=(clip, peer), device_id_type=MESH)

    def rw_copy(src, dst, slot, peer):
        return pltpu.make_async_remote_copy(
            src_ref=rw_ref.at[:, pl.ds(2 * src, 2)], dst_ref=rrw.at[dst],
            send_sem=rw_s.at[src], recv_sem=rw_r.at[slot],
            device_id=(clip, peer), device_id_type=MESH)

    own_in = pltpu.make_async_copy(x_ref.at[pl.ds(2 * me, 2)], rin.at[me], loc.at[0])
    own_rw = pltpu.make_async_copy(rw_ref.at[:, pl.ds(2 * me, 2)], rrw.at[me], loc.at[1])

    def start_in(i):
        peer = tile_peer(14 - i)
        in_copy(peer, me, me, peer).start()

    def start_rw(i):
        peer = tile_peer(14 - i)
        rw_copy(peer, me, me, peer).start()

    loop(15, start_rw)
    own_rw.start()
    loop(EARLY, start_in)
    own_in.start()

    low_peer, high_peer = (me + TILES - 1) % TILES, (me + 1) % TILES

    def halo_pair(ref, k):
        up = pltpu.make_async_remote_copy(
            src_ref=ref.at[2], dst_ref=ref.at[0],
            send_sem=halo_s.at[2 * k], recv_sem=halo_r.at[2 * k],
            device_id=(clip, high_peer), device_id_type=MESH)
        down = pltpu.make_async_remote_copy(
            src_ref=ref.at[1], dst_ref=ref.at[3],
            send_sem=halo_s.at[2 * k + 1], recv_sem=halo_r.at[2 * k + 1],
            device_id=(clip, low_peer), device_id_type=MESH)
        return up, down

    def put_halo(ref, y_ref):
        def body(f):
            put_row(y_ref, f, 0, jnp.where(me > 0, ref[0, f].astype(F32), 0.0).astype(BF16))
            put_row(y_ref, f, 3, jnp.where(me < TILES - 1, ref[3, f].astype(F32), 0.0).astype(BF16))

        loop(FRAMES, body)

    def rw_arrived(i):
        src = tile_peer(i)
        rw_copy(src, src, src, src).wait_recv()

    own_rw.wait()
    loop(15, rw_arrived)
    for i in range(C // 16):
        rows = slice(16 * i, 16 * i + 16)
        slots = jnp.concatenate(
            [rrw[:, :, h, rows, :].reshape(512, W) for h in range(2)], axis=1)
        got = jnp.dot(pick[...], slots, preferred_element_type=F32).astype(BF16)
        got = got.reshape(FRAMES, 16, 2 * W)
        xg4[1, :, rows, :] = got[:, :, :W]
        xg4[2, :, rows, :] = got[:, :, W:]
    halo = halo_pair(xg4, 0)
    for copy in halo:
        copy.start()
    loop(15 - EARLY, lambda i: start_in(i + EARLY))

    def put_own(f):
        for h in range(2):
            put_row(yg, f, 1 + h, xg4[1 + h, f])

    loop(FRAMES, put_own)
    for copy in halo:
        copy.wait()
    put_halo(xg4, yg)

    def conv(kernel_ref, y_ref, first, reverse, each):
        c1[...] = jnp.zeros_like(c1)
        c2[...] = jnp.zeros_like(c2)

        def frame(f, one, two):
            p = jnp.dot(kernel_ref[...], y_ref[f], preferred_element_type=F32)
            if first is not None:
                one, two = jnp.where(f == FRAMES - 1, 0.0, one), jnp.where(f == FRAMES - 1, 0.0, two)
            return p[2 * C:] + one, p[C:2 * C] + two, p[:C]

        if first is not None:
            zero = jnp.zeros((C, 2 * W), F32)
            _, one, two = frame((first + 2) % FRAMES, zero, zero)
            _, one, two = frame((first + 1) % FRAMES, one, two)
            c1[...] = one
            c2[...] = two

        def body(i):
            one, two = c1[...], c2[...]
            for k in range(UNROLL):
                f = i * UNROLL + k
                if first is not None:
                    f = (first + FRAMES - f) % FRAMES
                elif reverse:
                    f = FRAMES - 1 - f
                value, one, two = frame(f, one, two)
                each(f, value.astype(BF16))
            c1[...] = one
            c2[...] = two

        loop(FRAMES // UNROLL, body)

    def keep(f, g):
        gm[f] = g

    conv(k2t, yg, None, True, keep)

    def first(f):
        for h in range(2):
            v = norm_silu(rin[f, h].astype(F32), g1c[...]).astype(BF16)
            x4[1 + h, f] = v
            put_row(yin, f, 1 + h, v)

    own_in.wait()
    first(me)

    def arrived(i):
        src = tile_peer(i)
        in_copy(src, src, src, src).wait_recv()
        first(src)

    loop(15, arrived)
    halo = halo_pair(x4, 1)
    for copy in halo:
        copy.start()
    for copy in halo:
        copy.wait()
    put_halo(x4, yin)

    def mid(f, h):
        for row in range(2):
            lanes = slice(row * W, (row + 1) * W)
            v, g = mid_both(gm[f, :, lanes].astype(F32), h[:, lanes].astype(F32), g2c[...])
            act[f + 2, :, lanes] = v.astype(BF16)
            g = g.astype(BF16)
            xh4[1 + row, f] = g
            gh[f, :, lanes] = g
            put_row(yh, f, 1 + row, g)

    conv(k1f, yin, None, False, mid)
    halo = halo_pair(xh4, 2)
    for copy in halo:
        copy.start()

    mine, other = core * 64, (1 - core) * 64
    base = mine + 4 * clip

    def weight(n, left, y_ref):
        def body(i):
            total = w[n, :, :TAPS]
            for k in range(4):
                f = i * 4 + k
                rows = left(f)
                total = total + lax.dot_general(
                    rows, y_ref[f], (((1,), (1,)), ((), ())), preferred_element_type=F32)
            w[n, :, :TAPS] = total

        loop(FRAMES // 4, body)

        def pack(i):
            rows = w[n, pl.ds(pl.multiple_of(16 * i, 16), 16), :]
            for j in range(7):
                piece = rows[:, 128 * j:128 * (j + 1)]
                bb[n, 7 * i + j] = piece
                sb[n, 7 * i + j] = piece.astype(BF16)

        loop(18, pack)

    def s0_copy(n):
        return pltpu.make_async_remote_copy(
            src_ref=sb.at[n, pl.ds(other, 64)], dst_ref=r0.at[n],
            send_sem=s0_s.at[n], recv_sem=s0_r.at[n],
            device_id=(clip, sibling), device_id_type=MESH)

    def s1_copy(n, piece, slot_at, peer):
        return pltpu.make_async_remote_copy(
            src_ref=s1b.at[n, pl.ds(4 * piece, 4)], dst_ref=r1.at[n, slot_at],
            send_sem=s1_s.at[n, piece], recv_sem=s1_r.at[n, slot_at],
            device_id=(peer, me), device_id_type=MESH)

    def s2_copy(n, to, slot_at):
        return pltpu.make_async_remote_copy(
            src_ref=c16.at[n], dst_ref=r2.at[n, slot_at],
            send_sem=s2_s.at[n, to], recv_sem=s2_r.at[n, slot_at],
            device_id=(clip, 2 * to + core), device_id_type=MESH)

    def a1_copy(n, at, to):
        piece = res_ref.at[n, pl.ds(mine + 4 * at, 4)]
        return pltpu.make_async_remote_copy(
            src_ref=piece, dst_ref=piece,
            send_sem=a1_s.at[n, to], recv_sem=a1_r.at[n, at],
            device_id=(to, me), device_id_type=MESH)

    def a0_copy(n, half):
        piece = res_ref.at[n, pl.ds(half, 64)]
        return pltpu.make_async_remote_copy(
            src_ref=piece, dst_ref=piece, send_sem=a0_s.at[n], recv_sem=a0_r.at[n],
            device_id=(clip, sibling), device_id_type=MESH)

    def sum_pair(n):
        s0_copy(n).start()

    def sum_clips(n):
        s0_copy(n).wait()

        def add(i):
            at = pl.ds(4 * i, 4)
            s1b[n, at] = (
                bb[n, pl.ds(mine + 4 * i, 4)] + r0[n, at].astype(F32)).astype(BF16)

        loop(16, add)
        loop(15, lambda i: s1_copy(n, clip_peer(i), clip, clip_peer(i)).start())
        r1[n, clip] = s1b[n, pl.ds(4 * clip, 4)]

    def sum_z(n):
        loop(15, lambda i: s1_copy(n, clip_peer(i), clip_peer(i), clip_peer(i)).wait())

        def add(i):
            total = r1[n, 0, i].astype(F32)
            for p in range(1, CLIPS):
                total = total + r1[n, p, i].astype(F32)
            c16[n, i] = total.astype(BF16)

        loop(4, add)
        loop(7, lambda i: s2_copy(n, z_of(i), z).start())
        r2[n, z] = c16[n]

    def spread_clips(n):
        loop(7, lambda i: s2_copy(n, z_of(i), z_of(i)).wait())
        total = r2[n, 0].astype(F32)
        for p in range(1, 8):
            total = total + r2[n, p].astype(F32)
        res_ref[n, pl.ds(base, 4)] = total.astype(BF16)
        loop(15, lambda i: a1_copy(n, clip, clip_peer(i)).start())

    def spread_pair(n):
        def finish(i):
            a1_copy(n, clip_peer(i), clip_peer(i)).wait_recv()
            a1_copy(n, clip, clip_peer(i)).wait_send()

        loop(15, finish)
        a0_copy(n, mine).start()

    def finish_sum(n):
        a0_copy(n, other).wait_recv()
        a0_copy(n, mine).wait_send()

    weight(0, lambda f: jnp.concatenate([gh[f + 2], gh[f + 1], gh[f]], axis=0), yin)
    sum_pair(0)
    weight(1, lambda f: jnp.concatenate([act[f], act[f + 1], act[f + 2]], axis=0), yg)
    sum_pair(1)
    sum_clips(0)

    for copy in halo:
        copy.wait()
    put_halo(xh4, yh)
    sum_clips(1)

    def f_copy(f, dst_rows, slot_at, peer):
        return pltpu.make_async_remote_copy(
            src_ref=fb.at[f], dst_ref=out_ref.at[pl.ds(2 * dst_rows, 2)],
            send_sem=f_s.at[f], recv_sem=f_r.at[slot_at],
            device_id=(clip, peer), device_id_type=MESH)

    own_out = pltpu.make_async_copy(fb.at[me], out_ref.at[pl.ds(2 * me, 2)], loc.at[2])

    def back_in(f, g):
        for row in range(2):
            v = norm_backward(
                g[:, row * W:(row + 1) * W].astype(F32), rin[f, row].astype(F32), g1c[...])
            fb[f, row] = (xg4[1 + row, f].astype(F32) + v).astype(BF16)

        @pl.when(f != me)
        def _():
            f_copy(f, me, me, f).start()

        @pl.when(f == me)
        def _():
            own_out.start()

    conv(k1t, yh, (me + 8) % FRAMES, True, back_in)

    sum_z(0)
    sum_z(1)
    spread_clips(0)
    spread_clips(1)
    spread_pair(0)
    spread_pair(1)
    finish_sum(0)
    finish_sum(1)

    own_out.wait()

    def drain(i):
        peer = tile_peer(i)
        f_copy(peer, peer, peer, peer).wait_recv()
        f_copy(peer, me, me, peer).wait_send()
        in_copy(peer, me, me, peer).wait_send()
        rw_copy(peer, me, me, peer).wait_send()

    loop(15, drain)


def unpack(scale, p_ref, o1_ref, o2_ref, s_ref):
    for n, o_ref in enumerate((o1_ref, o2_ref)):
        def body(i, carry):
            for j in range(7):
                s_ref[pl.ds(pl.multiple_of(16 * i, 16), 16), 128 * j:128 * (j + 1)] = (
                    p_ref[n, 7 * i + j].astype(F32) * scale)
            return carry

        lax.fori_loop(0, 18, body, 0)
        for a in range(3):
            for i in range(9):
                block = s_ref[a * C:(a + 1) * C, i * C:(i + 1) * C]
                if n == 0:
                    o_ref[a * 9 + i] = block
                else:
                    o_ref[a * 9 + 8 - i] = jnp.transpose(block)


def local(
    decoder_input, reward_grad, reward_owner, scored_frame,
    first_gain, second_gain, first_kernel, second_kernel,
):
    vmem = pl.BlockSpec(memory_space=pltpu.VMEM)
    hbm = pl.BlockSpec(memory_space=pl.ANY)
    dma = pltpu.SemaphoreType.DMA
    feature, packed = pl.pallas_call(
        kernel,
        out_shape=(
            jax.ShapeDtypeStruct((32, C, W), BF16),
            jax.ShapeDtypeStruct((2, 128, 16, 128), BF16),
        ),
        in_specs=[hbm, hbm] + [vmem] * 6,
        out_specs=(hbm, vmem),
        scratch_shapes=[
            pltpu.VMEM((16, 2, C, W), BF16),
            pltpu.VMEM((16, 2, 2, C, W), BF16),
            pltpu.VMEM((3 * C, TAPS), BF16),
            pltpu.VMEM((3 * C, TAPS), BF16),
            pltpu.VMEM((3 * C, TAPS), BF16),
            pltpu.VMEM((C, W), F32),
            pltpu.VMEM((C, W), F32),
            pltpu.VMEM((256, 512), BF16),
            pltpu.VMEM((4, 16, C, W), BF16),
            pltpu.VMEM((4, 16, C, W), BF16),
            pltpu.VMEM((4, 16, C, W), BF16),
            pltpu.VMEM((16, TAPS, 2 * W), BF16),
            pltpu.VMEM((16, TAPS, 2 * W), BF16),
            pltpu.VMEM((16, TAPS, 2 * W), BF16),
            pltpu.VMEM((16, C, 2 * W), BF16),
            pltpu.VMEM((18, C, 2 * W), BF16),
            pltpu.VMEM((18, C, 2 * W), BF16),
            pltpu.VMEM((C, 2 * W), F32),
            pltpu.VMEM((C, 2 * W), F32),
            pltpu.VMEM((16, 2, C, W), BF16),
            pltpu.VMEM((2, 3 * C, PADDED), F32),
            pltpu.VMEM((2, 128, 16, 128), F32),
            pltpu.VMEM((2, 128, 16, 128), BF16),
            pltpu.VMEM((2, 64, 16, 128), BF16),
            pltpu.VMEM((2, 64, 16, 128), BF16),
            pltpu.VMEM((2, 16, 4, 16, 128), BF16),
            pltpu.VMEM((2, 4, 16, 128), BF16),
            pltpu.VMEM((2, 8, 4, 16, 128), BF16),
            dma((16,)), dma((16,)), dma((16,)), dma((16,)), dma((3,)),
            dma((6,)), dma((6,)), dma((16,)), dma((16,)),
            dma((2,)), dma((2,)), dma((2, 16)), dma((2, 16)), dma((2, 8)), dma((2, 8)),
            dma((2, 16)), dma((2, 16)), dma((2,)), dma((2,)),
        ],
        compiler_params=pltpu.CompilerParams(
            collective_id=0, has_side_effects=True, vmem_limit_bytes=60 * 2**20),
    )(
        decoder_input[0, 0],
        reward_grad[0],
        reward_owner[0].reshape(1, 16),
        scored_frame,
        first_gain.reshape(1, C),
        second_gain.reshape(1, C),
        first_kernel.reshape(27, C, C),
        second_kernel.reshape(27, C, C),
    )
    first_total, second_total = pl.pallas_call(
        functools.partial(unpack, 1.0 / 1024.0),
        out_shape=(jax.ShapeDtypeStruct((27, C, C), F32),) * 2,
        in_specs=[vmem],
        out_specs=(vmem, vmem),
        scratch_shapes=[pltpu.VMEM((3 * C, PADDED), F32)],
        compiler_params=pltpu.CompilerParams(vmem_limit_bytes=32 * 2**20),
    )(packed)
    shape = (3, 3, 3, C, C)
    return feature[None, None], first_total.reshape(shape), second_total.reshape(shape)


def solution(mesh):
    in_specs = (
        P("clip", "tile", None, None, None),
        P("clip", "tile", None, None, None),
        P("clip", None, None),
        P("clip", None),
        P(),
        P(),
        P(),
        P(),
    )
    out_specs = (P("clip", "tile", None, None, None), P(), P())
    return jax.shard_map(local, mesh=mesh, in_specs=in_specs, out_specs=out_specs, check_vma=False)
```

```python
import functools

import jax
import jax.numpy as jnp
from jax import lax
from jax.experimental import pallas as pl
from jax.experimental.pallas import tpu as pltpu
from jax.sharding import PartitionSpec as P

MESH = pl.DeviceIdType.MESH
F32 = jnp.float32
BF16 = jnp.bfloat16
epsilon = 1e-06

FRAMES = 16
TILES = 16
CLIPS = 16
C = 96
W = 128
TAPS = 9 * C
PADDED = 896
UNROLL = 2
EARLY = 15
HELD = 10
CHUNK = 4


def inverse_rms(x):
    return lax.rsqrt(jnp.mean(x * x, axis=0, keepdims=True) + epsilon)


def sigmoid(u):
    return 0.5 * jnp.tanh(0.5 * u) + 0.5


def norm_silu(x, gain):
    u = gain * (x * inverse_rms(x))
    return u * sigmoid(u)


def norm_backward(g, x, gain):
    r = inverse_rms(x)
    normed = x * r
    u = gain * normed
    sig = sigmoid(u)
    q = g * gain * sig * (1.0 + u * (1.0 - sig))
    p = jnp.mean(q * normed, axis=0, keepdims=True)
    return r * (q - normed * p)


def mid_both(g, x, gain):
    r = inverse_rms(x)
    normed = x * r
    u = gain * normed
    sig = sigmoid(u)
    q = g * gain * sig * (1.0 + u * (1.0 - sig))
    p = jnp.mean(q * normed, axis=0, keepdims=True)
    return u * sig, r * (q - normed * p)


def put_row(y_ref, f, r, value):
    lane = lax.broadcasted_iota(jnp.int32, (C, W), 1)
    wide = value.astype(F32)
    low = jnp.where(lane == 0, 0.0, pltpu.roll(wide, 1, 1)).astype(BF16)
    high = jnp.where(lane == W - 1, 0.0, pltpu.roll(wide, W - 1, 1)).astype(BF16)
    for e, v in enumerate((low, value, high)):
        for b in range(3):
            h = r - b
            if 0 <= h < 2:
                y_ref[f, (b * 3 + e) * C:(b * 3 + e + 1) * C, h * W:(h + 1) * W] = v


def kernel(
    x_ref, rw_ref, own_ref, scored_ref, g1_ref, g2_ref, k1_ref, k2_ref,
    out_ref, res_ref,
    rin, rrw, k1f, k1t, k2t, g1c, g2c, pick,
    x4, xg4, xh4, yin, yg, yh, gm, act, gh, c1, c2, fb,
    w, bb, sb, r0, s1b, r1, c16, r2,
    in_s, in_r, rw_s, rw_r, loc, halo_s, halo_r, x_s, x_r, f_s, f_r,
    s0_s, s0_r, s1_s, s1_r, s2_s, s2_r, a1_s, a1_r, a0_s, a0_r,
):
    clip = lax.axis_index("clip")
    me = lax.axis_index("tile")
    core = me % 2
    z = me // 2
    sibling = me + 1 - 2 * core

    def tile_peer(i):
        step = i // 2 + 1
        return (me + (1 - i % 2) * step + (i % 2) * (TILES - step)) % TILES

    def clip_peer(i):
        return (clip + i + 1) % CLIPS

    def z_of(i):
        return (z + i + 1) % 8

    def loop(n, body):
        def step(i, carry):
            body(i)
            return carry

        lax.fori_loop(0, n, step, 0)

    barrier = pltpu.get_barrier_semaphore()
    loop(15, lambda i: pl.semaphore_signal(
        barrier, inc=1, device_id=(clip, tile_peer(i)), device_id_type=MESH))
    loop(15, lambda i: pl.semaphore_signal(
        barrier, inc=1, device_id=(clip_peer(i), me), device_id_type=MESH))

    def column(row, n, zero):
        eye = (lax.broadcasted_iota(jnp.int32, (n, n), 0)
               == lax.broadcasted_iota(jnp.int32, (n, n), 1))
        return jnp.sum(jnp.where(eye, jnp.broadcast_to(row, (n, n)), zero), axis=1, keepdims=True)

    g1c[...] = jnp.broadcast_to(column(g1_ref[...], C, 0.0), (C, W))
    g2c[...] = jnp.broadcast_to(column(g2_ref[...], C, 0.0), (C, W))

    own_row = own_ref[...]
    own_col = column(own_row, 16, 0)
    earlier = (lax.broadcasted_iota(jnp.int32, (16, 16), 1)
               < lax.broadcasted_iota(jnp.int32, (16, 16), 0))
    same = own_col == own_row
    ranking = jnp.sum(jnp.where(same & earlier, 1, 0), axis=1, keepdims=True)
    slot = own_col * 2 + ranking
    by_slot = jnp.where(
        slot == lax.shift_right_logical(lax.broadcasted_iota(jnp.int32, (16, 512), 1), 4),
        1.0, 0.0)
    by_frame = jnp.where(
        scored_ref[...]
        == lax.shift_right_logical(lax.broadcasted_iota(jnp.int32, (256, 16), 0), 4),
        1.0, 0.0)
    table = jnp.dot(by_frame, by_slot, preferred_element_type=F32)
    row16 = lax.broadcasted_iota(jnp.int32, (256, 512), 0) & 15
    col16 = lax.broadcasted_iota(jnp.int32, (256, 512), 1) & 15
    pick[...] = jnp.where(row16 == col16, table, 0.0).astype(BF16)

    for a in range(3):
        rows = slice(a * C, (a + 1) * C)
        k1f[rows, :] = jnp.concatenate(
            [k1_ref[a * 9 + i].astype(F32) for i in range(9)], axis=1).astype(BF16)
        k1t[rows, :] = jnp.transpose(jnp.concatenate(
            [k1_ref[a * 9 + 8 - i] for i in range(9)], axis=0).astype(F32)).astype(BF16)
        k2t[rows, :] = jnp.transpose(jnp.concatenate(
            [k2_ref[a * 9 + 8 - i] for i in range(9)], axis=0).astype(F32)).astype(BF16)

    act[0:2] = jnp.zeros((2, C, 2 * W), BF16)
    gh[16:18] = jnp.zeros((2, C, 2 * W), BF16)
    w[...] = jnp.zeros_like(w)
    for n in range(2):
        bb[n, 126:128] = jnp.zeros((2, 16, 128), F32)
        sb[n, 126:128] = jnp.zeros((2, 16, 128), BF16)

    pl.semaphore_wait(barrier, 30)

    def in_copy(src, dst, slot, peer):
        return pltpu.make_async_remote_copy(
            src_ref=x_ref.at[pl.ds(2 * src, 2)], dst_ref=rin.at[dst],
            send_sem=in_s.at[src], recv_sem=in_r.at[slot],
            device_id=(clip, peer), device_id_type=MESH)

    def rw_copy(src, dst, slot, peer):
        return pltpu.make_async_remote_copy(
            src_ref=rw_ref.at[:, pl.ds(2 * src, 2)], dst_ref=rrw.at[dst],
            send_sem=rw_s.at[src], recv_sem=rw_r.at[slot],
            device_id=(clip, peer), device_id_type=MESH)

    own_in = pltpu.make_async_copy(x_ref.at[pl.ds(2 * me, 2)], rin.at[me], loc.at[0])
    own_rw = pltpu.make_async_copy(rw_ref.at[:, pl.ds(2 * me, 2)], rrw.at[me], loc.at[1])

    def start_in(i):
        peer = tile_peer(14 - i)
        in_copy(peer, me, me, peer).start()

    def start_rw(i):
        peer = tile_peer(14 - i)
        rw_copy(peer, me, me, peer).start()

    loop(15, start_rw)
    own_rw.start()
    loop(EARLY, start_in)
    own_in.start()

    low_peer, high_peer = (me + TILES - 1) % TILES, (me + 1) % TILES

    def halo_pair(ref, k):
        up = pltpu.make_async_remote_copy(
            src_ref=ref.at[2], dst_ref=ref.at[0],
            send_sem=halo_s.at[2 * k], recv_sem=halo_r.at[2 * k],
            device_id=(clip, high_peer), device_id_type=MESH)
        down = pltpu.make_async_remote_copy(
            src_ref=ref.at[1], dst_ref=ref.at[3],
            send_sem=halo_s.at[2 * k + 1], recv_sem=halo_r.at[2 * k + 1],
            device_id=(clip, low_peer), device_id_type=MESH)
        return up, down

    def put_halo(ref, y_ref, f):
        put_row(y_ref, f, 0, jnp.where(me > 0, ref[0, f].astype(F32), 0.0).astype(BF16))
        put_row(y_ref, f, 3, jnp.where(me < TILES - 1, ref[3, f].astype(F32), 0.0).astype(BF16))

    def x_pair(c):
        at = pl.ds(CHUNK * c, CHUNK)
        up = pltpu.make_async_remote_copy(
            src_ref=x4.at[2, at], dst_ref=x4.at[0, at],
            send_sem=x_s.at[2 * c], recv_sem=x_r.at[2 * c],
            device_id=(clip, high_peer), device_id_type=MESH)
        down = pltpu.make_async_remote_copy(
            src_ref=x4.at[1, at], dst_ref=x4.at[3, at],
            send_sem=x_s.at[2 * c + 1], recv_sem=x_r.at[2 * c + 1],
            device_id=(clip, low_peer), device_id_type=MESH)
        return up, down

    def rw_arrived(i):
        src = tile_peer(i)
        rw_copy(src, src, src, src).wait_recv()

    own_rw.wait()
    loop(15, rw_arrived)
    for i in range(C // 16):
        rows = slice(16 * i, 16 * i + 16)
        slots = jnp.concatenate(
            [rrw[:, :, h, rows, :].reshape(512, W) for h in range(2)], axis=1)
        got = jnp.dot(pick[...], slots, preferred_element_type=F32).astype(BF16)
        got = got.reshape(FRAMES, 16, 2 * W)
        xg4[1, :, rows, :] = got[:, :, :W]
        xg4[2, :, rows, :] = got[:, :, W:]
    halo = halo_pair(xg4, 0)
    for copy in halo:
        copy.start()
    loop(15 - EARLY, lambda i: start_in(i + EARLY))

    def put_own(f):
        for h in range(2):
            put_row(yg, f, 1 + h, xg4[1 + h, f])

    loop(FRAMES, put_own)

    def conv(kernel_ref, y_ref, first, each):
        c1[...] = jnp.zeros_like(c1)
        c2[...] = jnp.zeros_like(c2)

        def frame(f, one, two):
            p = jnp.dot(kernel_ref[...], y_ref[f], preferred_element_type=F32)
            if first is not None:
                one, two = jnp.where(f == FRAMES - 1, 0.0, one), jnp.where(f == FRAMES - 1, 0.0, two)
            return p[2 * C:] + one, p[C:2 * C] + two, p[:C]

        if first is not None:
            zero = jnp.zeros((C, 2 * W), F32)
            _, one, two = frame((first + 2) % FRAMES, zero, zero)
            _, one, two = frame((first + 1) % FRAMES, one, two)
            c1[...] = one
            c2[...] = two

        def body(i):
            one, two = c1[...], c2[...]
            for k in range(UNROLL):
                step = i * UNROLL + k
                f = step
                if first is not None:
                    f = (first + FRAMES - f) % FRAMES
                else:
                    f = FRAMES - 1 - f
                value, one, two = frame(f, one, two)
                each(step, f, value.astype(BF16))
            c1[...] = one
            c2[...] = two

        loop(FRAMES // UNROLL, body)

    def keep(step, f, g):
        gm[f] = g

    def first(f):
        for h in range(2):
            v = norm_silu(rin[f, h].astype(F32), g1c[...]).astype(BF16)
            x4[1 + h, f] = v
            put_row(yin, f, 1 + h, v)

    own_in.wait()
    first(me)

    def arrived(i):
        src = tile_peer(i)
        in_copy(src, src, src, src).wait_recv()
        first(src)

    loop(15, arrived)

    def send_x(c):
        for copy in x_pair(c):
            copy.start()

    loop(FRAMES // CHUNK, send_x)

    for copy in halo:
        copy.wait()
    loop(FRAMES, lambda f: put_halo(xg4, yg, f))
    conv(k2t, yg, None, keep)

    def mid(f, h):
        for row in range(2):
            lanes = slice(row * W, (row + 1) * W)
            v, g = mid_both(gm[f, :, lanes].astype(F32), h[:, lanes].astype(F32), g2c[...])
            act[f + 2, :, lanes] = v.astype(BF16)
            g = g.astype(BF16)
            xh4[1 + row, f] = g
            gh[f, :, lanes] = g
            put_row(yh, f, 1 + row, g)

    c1[...] = jnp.zeros_like(c1)
    c2[...] = jnp.zeros_like(c2)

    def chunk(c):
        for copy in x_pair(c):
            copy.wait()
        for k in range(CHUNK):
            put_halo(x4, yin, c * CHUNK + k)
        one, two = c1[...], c2[...]
        for k in range(CHUNK):
            f = c * CHUNK + k
            p = jnp.dot(k1f[...], yin[f], preferred_element_type=F32)
            mid(f, (p[2 * C:] + one).astype(BF16))
            one = p[C:2 * C] + two
            two = p[:C]
        c1[...] = one
        c2[...] = two

    loop(FRAMES // CHUNK, chunk)
    halo = halo_pair(xh4, 1)
    for copy in halo:
        copy.start()

    mine, other = core * 64, (1 - core) * 64

    def weight(n, left, y_ref):
        def body(i):
            total = w[n, :, :TAPS]
            for k in range(4):
                f = i * 4 + k
                rows = left(f)
                total = total + lax.dot_general(
                    rows, y_ref[f], (((1,), (1,)), ((), ())), preferred_element_type=F32)
            w[n, :, :TAPS] = total

        loop(FRAMES // 4, body)

        def pack(i):
            rows = w[n, pl.ds(pl.multiple_of(16 * i, 16), 16), :]
            for j in range(7):
                piece = rows[:, 128 * j:128 * (j + 1)]
                bb[n, 7 * i + j] = piece
                sb[n, 7 * i + j] = piece.astype(BF16)

        loop(18, pack)

    def s0_copy(n, piece):
        return pltpu.make_async_remote_copy(
            src_ref=sb.at[n, pl.ds(other + 4 * piece, 4)], dst_ref=r0.at[n, pl.ds(4 * piece, 4)],
            send_sem=s0_s.at[n, piece], recv_sem=s0_r.at[n, piece],
            device_id=(clip, sibling), device_id_type=MESH)

    def s1_copy(n, piece, slot_at, peer):
        return pltpu.make_async_remote_copy(
            src_ref=s1b.at[n, pl.ds(4 * piece, 4)], dst_ref=r1.at[n, slot_at],
            send_sem=s1_s.at[n, piece], recv_sem=s1_r.at[n, slot_at],
            device_id=(peer, me), device_id_type=MESH)

    def s2_copy(to, slot_at):
        return pltpu.make_async_remote_copy(
            src_ref=c16, dst_ref=r2.at[slot_at],
            send_sem=s2_s.at[to], recv_sem=s2_r.at[slot_at],
            device_id=(clip, 2 * to + core), device_id_type=MESH)

    def a1_copy(at, to):
        piece = res_ref.at[16 * core + at]
        return pltpu.make_async_remote_copy(
            src_ref=piece, dst_ref=piece,
            send_sem=a1_s.at[to], recv_sem=a1_r.at[at],
            device_id=(to, me), device_id_type=MESH)

    def a0_copy(half, at):
        piece = res_ref.at[16 * half + at]
        return pltpu.make_async_remote_copy(
            src_ref=piece, dst_ref=piece, send_sem=a0_s.at[at], recv_sem=a0_r.at[at],
            device_id=(clip, sibling), device_id_type=MESH)

    def sum_pair(n):
        loop(16, lambda i: s0_copy(n, clip_peer(i)).start())

    def sum_clips(n):
        def piece_of(p):
            s0_copy(n, p).wait()
            return (bb[n, pl.ds(mine + 4 * p, 4)]
                    + r0[n, pl.ds(4 * p, 4)].astype(F32)).astype(BF16)

        def add(i):
            p = clip_peer(i)
            s1b[n, pl.ds(4 * p, 4)] = piece_of(p)
            s1_copy(n, p, clip, p).start()

        loop(15, add)
        r1[n, clip] = piece_of(clip)

    def sum_z():
        for n in range(2):
            loop(15, lambda i: s1_copy(n, clip_peer(i), clip_peer(i), clip_peer(i)).wait())

            def add(i):
                total = r1[n, 0, i].astype(F32)
                for p in range(1, CLIPS):
                    total = total + r1[n, p, i].astype(F32)
                c16[4 * n + i] = total.astype(BF16)

            loop(4, add)
        loop(7, lambda i: s2_copy(z_of(i), z).start())
        r2[z] = c16[...]

    def spread_clips():
        loop(7, lambda i: s2_copy(z_of(i), z_of(i)).wait())
        total = r2[0].astype(F32)
        for p in range(1, 8):
            total = total + r2[p].astype(F32)
        res_ref[16 * core + clip] = total.astype(BF16)
        loop(15, lambda i: a1_copy(clip, clip_peer(i)).start())
        a0_copy(core, clip).start()

    def spread_pair():
        def forward(i):
            p = clip_peer(i)
            a1_copy(p, p).wait_recv()
            a0_copy(core, p).start()

        loop(15, forward)

    def finish_sum():
        loop(15, lambda i: a1_copy(clip, clip_peer(i)).wait_send())
        loop(16, lambda i: a0_copy(1 - core, i).wait_recv())
        loop(16, lambda i: a0_copy(core, i).wait_send())

    weight(0, lambda f: jnp.concatenate([gh[f + 2], gh[f + 1], gh[f]], axis=0), yin)
    sum_pair(0)
    weight(1, lambda f: jnp.concatenate([act[f], act[f + 1], act[f + 2]], axis=0), yg)
    sum_pair(1)
    for copy in halo:
        copy.wait()
    loop(FRAMES, lambda f: put_halo(xh4, yh, f))
    sum_clips(0)
    sum_clips(1)

    def f_copy(f, dst_rows, slot_at, peer):
        return pltpu.make_async_remote_copy(
            src_ref=fb.at[f], dst_ref=out_ref.at[pl.ds(2 * dst_rows, 2)],
            send_sem=f_s.at[f], recv_sem=f_r.at[slot_at],
            device_id=(clip, peer), device_id_type=MESH)

    own_out = pltpu.make_async_copy(fb.at[me], out_ref.at[pl.ds(2 * me, 2)], loc.at[2])

    def back_in(step, f, g):
        for row in range(2):
            v = norm_backward(
                g[:, row * W:(row + 1) * W].astype(F32), rin[f, row].astype(F32), g1c[...])
            fb[f, row] = (xg4[1 + row, f].astype(F32) + v).astype(BF16)

        @pl.when((f != me) & (step < FRAMES - HELD))
        def _():
            f_copy(f, me, me, f).start()

        @pl.when(f == me)
        def _():
            own_out.start()

    conv(k1t, yh, (me + 8) % FRAMES, back_in)

    sum_z()

    def send_held(i):
        f = (me + 8 + HELD - i) % FRAMES

        @pl.when(f != me)
        def _():
            f_copy(f, me, me, f).start()

    loop(HELD, send_held)
    spread_clips()
    spread_pair()
    finish_sum()

    own_out.wait()

    def drain(i):
        peer = tile_peer(i)
        f_copy(peer, peer, peer, peer).wait_recv()
        f_copy(peer, me, me, peer).wait_send()
        in_copy(peer, me, me, peer).wait_send()
        rw_copy(peer, me, me, peer).wait_send()

    loop(15, drain)


def unpack(scale, p_ref, o1_ref, o2_ref, s_ref):
    for n, o_ref in enumerate((o1_ref, o2_ref)):
        def body(i, carry):
            for j in range(7):
                s_ref[pl.ds(pl.multiple_of(16 * i, 16), 16), 128 * j:128 * (j + 1)] = (
                    p_ref[(7 * i + j) // 4, 4 * n + (7 * i + j) % 4].astype(F32) * scale)
            return carry

        lax.fori_loop(0, 18, body, 0)
        for a in range(3):
            for i in range(9):
                block = s_ref[a * C:(a + 1) * C, i * C:(i + 1) * C]
                if n == 0:
                    o_ref[a * 9 + i] = block
                else:
                    o_ref[a * 9 + 8 - i] = jnp.transpose(block)


def local(
    decoder_input, reward_grad, reward_owner, scored_frame,
    first_gain, second_gain, first_kernel, second_kernel,
):
    vmem = pl.BlockSpec(memory_space=pltpu.VMEM)
    hbm = pl.BlockSpec(memory_space=pl.ANY)
    dma = pltpu.SemaphoreType.DMA
    feature, packed = pl.pallas_call(
        kernel,
        out_shape=(
            jax.ShapeDtypeStruct((32, C, W), BF16),
            jax.ShapeDtypeStruct((32, 8, 16, 128), BF16),
        ),
        in_specs=[hbm, hbm] + [vmem] * 6,
        out_specs=(hbm, vmem),
        scratch_shapes=[
            pltpu.VMEM((16, 2, C, W), BF16),
            pltpu.VMEM((16, 2, 2, C, W), BF16),
            pltpu.VMEM((3 * C, TAPS), BF16),
            pltpu.VMEM((3 * C, TAPS), BF16),
            pltpu.VMEM((3 * C, TAPS), BF16),
            pltpu.VMEM((C, W), F32),
            pltpu.VMEM((C, W), F32),
            pltpu.VMEM((256, 512), BF16),
            pltpu.VMEM((4, 16, C, W), BF16),
            pltpu.VMEM((4, 16, C, W), BF16),
            pltpu.VMEM((4, 16, C, W), BF16),
            pltpu.VMEM((16, TAPS, 2 * W), BF16),
            pltpu.VMEM((16, TAPS, 2 * W), BF16),
            pltpu.VMEM((16, TAPS, 2 * W), BF16),
            pltpu.VMEM((16, C, 2 * W), BF16),
            pltpu.VMEM((18, C, 2 * W), BF16),
            pltpu.VMEM((18, C, 2 * W), BF16),
            pltpu.VMEM((C, 2 * W), F32),
            pltpu.VMEM((C, 2 * W), F32),
            pltpu.VMEM((16, 2, C, W), BF16),
            pltpu.VMEM((2, 3 * C, PADDED), F32),
            pltpu.VMEM((2, 128, 16, 128), F32),
            pltpu.VMEM((2, 128, 16, 128), BF16),
            pltpu.VMEM((2, 64, 16, 128), BF16),
            pltpu.VMEM((2, 64, 16, 128), BF16),
            pltpu.VMEM((2, 16, 4, 16, 128), BF16),
            pltpu.VMEM((8, 16, 128), BF16),
            pltpu.VMEM((8, 8, 16, 128), BF16),
            dma((16,)), dma((16,)), dma((16,)), dma((16,)), dma((3,)),
            dma((4,)), dma((4,)), dma((8,)), dma((8,)), dma((16,)), dma((16,)),
            dma((2, 16)), dma((2, 16)), dma((2, 16)), dma((2, 16)), dma((8,)), dma((8,)),
            dma((16,)), dma((16,)), dma((16,)), dma((16,)),
        ],
        compiler_params=pltpu.CompilerParams(
            collective_id=0, has_side_effects=True, vmem_limit_bytes=60 * 2**20),
    )(
        decoder_input[0, 0],
        reward_grad[0],
        reward_owner[0].reshape(1, 16),
        scored_frame,
        first_gain.reshape(1, C),
        second_gain.reshape(1, C),
        first_kernel.reshape(27, C, C),
        second_kernel.reshape(27, C, C),
    )
    first_total, second_total = pl.pallas_call(
        functools.partial(unpack, 1.0 / 1024.0),
        out_shape=(jax.ShapeDtypeStruct((27, C, C), F32),) * 2,
        in_specs=[vmem],
        out_specs=(vmem, vmem),
        scratch_shapes=[pltpu.VMEM((3 * C, PADDED), F32)],
        compiler_params=pltpu.CompilerParams(vmem_limit_bytes=32 * 2**20),
    )(packed)
    shape = (3, 3, 3, C, C)
    return feature[None, None], first_total.reshape(shape), second_total.reshape(shape)


def solution(mesh):
    in_specs = (
        P("clip", "tile", None, None, None),
        P("clip", "tile", None, None, None),
        P("clip", None, None),
        P("clip", None),
        P(),
        P(),
        P(),
        P(),
    )
    out_specs = (P("clip", "tile", None, None, None), P(), P())
    return jax.shard_map(local, mesh=mesh, in_specs=in_specs, out_specs=out_specs, check_vma=False)
```

```python
import functools

import jax
import jax.numpy as jnp
from jax import lax
from jax.experimental import pallas as pl
from jax.experimental.pallas import tpu as pltpu
from jax.sharding import PartitionSpec as P

MESH = pl.DeviceIdType.MESH
F32 = jnp.float32
BF16 = jnp.bfloat16
epsilon = 1e-06

FRAMES = 16
TILES = 16
CLIPS = 16
C = 96
W = 128
TAPS = 9 * C
PADDED = 896
UNROLL = 4
EARLY = 15
HELD = 13
CHUNK = 4


def inverse_rms(x):
    return lax.rsqrt(jnp.mean(x * x, axis=0, keepdims=True) + epsilon)


def sigmoid(u):
    return 0.5 * jnp.tanh(0.5 * u) + 0.5


def norm_silu(x, gain):
    u = gain * (x * inverse_rms(x))
    return u * sigmoid(u)


def norm_backward(g, x, gain):
    r = inverse_rms(x)
    normed = x * r
    u = gain * normed
    sig = sigmoid(u)
    q = g * gain * sig * (1.0 + u * (1.0 - sig))
    p = jnp.mean(q * normed, axis=0, keepdims=True)
    return r * (q - normed * p)


def mid_both(g, x, gain):
    r = inverse_rms(x)
    normed = x * r
    u = gain * normed
    sig = sigmoid(u)
    q = g * gain * sig * (1.0 + u * (1.0 - sig))
    p = jnp.mean(q * normed, axis=0, keepdims=True)
    return u * sig, r * (q - normed * p)


def put_row(y_ref, f, r, value):
    lane = lax.broadcasted_iota(jnp.int32, (C, W), 1)
    wide = value.astype(F32)
    low = jnp.where(lane == 0, 0.0, pltpu.roll(wide, 1, 1)).astype(BF16)
    high = jnp.where(lane == W - 1, 0.0, pltpu.roll(wide, W - 1, 1)).astype(BF16)
    for e, v in enumerate((low, value, high)):
        for b in range(3):
            h = r - b
            if 0 <= h < 2:
                y_ref[f, (b * 3 + e) * C:(b * 3 + e + 1) * C, h * W:(h + 1) * W] = v


def kernel(
    x_ref, rw_ref, own_ref, scored_ref, g1_ref, g2_ref, k1_ref, k2_ref,
    out_ref, res_ref,
    rin, rrw, k1f, k1t, k2t, g1c, g2c, pick,
    x4, xg4, xh4, yin, yg, yh, gm, act, gh, c1, c2, fb,
    w, bb, sb, r0, s1b, r1, c16, r2,
    in_s, in_r, rw_s, rw_r, loc, halo_s, halo_r, x_s, x_r, f_s, f_r,
    s0_s, s0_r, s1_s, s1_r, s2_s, s2_r, a1_s, a1_r, a0_s, a0_r,
):
    clip = lax.axis_index("clip")
    me = lax.axis_index("tile")
    core = me % 2
    z = me // 2
    sibling = me + 1 - 2 * core

    def tile_peer(i):
        step = i // 2 + 1
        return (me + (1 - i % 2) * step + (i % 2) * (TILES - step)) % TILES

    def clip_peer(i):
        return (clip + i + 1) % CLIPS

    def z_of(i):
        return (z + i + 1) % 8

    def loop(n, body):
        def step(i, carry):
            body(i)
            return carry

        lax.fori_loop(0, n, step, 0)

    barrier = pltpu.get_barrier_semaphore()
    loop(15, lambda i: pl.semaphore_signal(
        barrier, inc=1, device_id=(clip, tile_peer(i)), device_id_type=MESH))
    loop(15, lambda i: pl.semaphore_signal(
        barrier, inc=1, device_id=(clip_peer(i), me), device_id_type=MESH))

    def column(row, n, zero):
        eye = (lax.broadcasted_iota(jnp.int32, (n, n), 0)
               == lax.broadcasted_iota(jnp.int32, (n, n), 1))
        return jnp.sum(jnp.where(eye, jnp.broadcast_to(row, (n, n)), zero), axis=1, keepdims=True)

    g1c[...] = jnp.broadcast_to(column(g1_ref[...], C, 0.0), (C, W))
    g2c[...] = jnp.broadcast_to(column(g2_ref[...], C, 0.0), (C, W))

    own_row = own_ref[...]
    own_col = column(own_row, 16, 0)
    earlier = (lax.broadcasted_iota(jnp.int32, (16, 16), 1)
               < lax.broadcasted_iota(jnp.int32, (16, 16), 0))
    same = own_col == own_row
    ranking = jnp.sum(jnp.where(same & earlier, 1, 0), axis=1, keepdims=True)
    slot = own_col * 2 + ranking
    by_slot = jnp.where(
        slot == lax.shift_right_logical(lax.broadcasted_iota(jnp.int32, (16, 512), 1), 4),
        1.0, 0.0)
    by_frame = jnp.where(
        scored_ref[...]
        == lax.shift_right_logical(lax.broadcasted_iota(jnp.int32, (256, 16), 0), 4),
        1.0, 0.0)
    table = jnp.dot(by_frame, by_slot, preferred_element_type=F32)
    row16 = lax.broadcasted_iota(jnp.int32, (256, 512), 0) & 15
    col16 = lax.broadcasted_iota(jnp.int32, (256, 512), 1) & 15
    pick[...] = jnp.where(row16 == col16, table, 0.0).astype(BF16)

    for a in range(3):
        rows = slice(a * C, (a + 1) * C)
        k1f[rows, :] = jnp.concatenate(
            [k1_ref[a * 9 + i].astype(F32) for i in range(9)], axis=1).astype(BF16)
        k1t[rows, :] = jnp.transpose(jnp.concatenate(
            [k1_ref[a * 9 + 8 - i] for i in range(9)], axis=0).astype(F32)).astype(BF16)
        k2t[rows, :] = jnp.transpose(jnp.concatenate(
            [k2_ref[a * 9 + 8 - i] for i in range(9)], axis=0).astype(F32)).astype(BF16)

    act[0:2] = jnp.zeros((2, C, 2 * W), BF16)
    gh[16:18] = jnp.zeros((2, C, 2 * W), BF16)
    w[...] = jnp.zeros_like(w)
    for n in range(2):
        bb[n, 126:128] = jnp.zeros((2, 16, 128), F32)
        sb[n, 126:128] = jnp.zeros((2, 16, 128), BF16)

    pl.semaphore_wait(barrier, 30)

    def in_copy(src, dst, slot, peer):
        return pltpu.make_async_remote_copy(
            src_ref=x_ref.at[pl.ds(2 * src, 2)], dst_ref=rin.at[dst],
            send_sem=in_s.at[src], recv_sem=in_r.at[slot],
            device_id=(clip, peer), device_id_type=MESH)

    def rw_copy(src, dst, slot, peer):
        return pltpu.make_async_remote_copy(
            src_ref=rw_ref.at[:, pl.ds(2 * src, 2)], dst_ref=rrw.at[dst],
            send_sem=rw_s.at[src], recv_sem=rw_r.at[slot],
            device_id=(clip, peer), device_id_type=MESH)

    own_in = pltpu.make_async_copy(x_ref.at[pl.ds(2 * me, 2)], rin.at[me], loc.at[0])
    own_rw = pltpu.make_async_copy(rw_ref.at[:, pl.ds(2 * me, 2)], rrw.at[me], loc.at[1])

    def start_in(i):
        peer = tile_peer(14 - i)
        in_copy(peer, me, me, peer).start()

    def start_rw(i):
        peer = tile_peer(14 - i)
        rw_copy(peer, me, me, peer).start()

    loop(15, start_rw)
    own_rw.start()
    loop(EARLY, start_in)
    own_in.start()

    low_peer, high_peer = (me + TILES - 1) % TILES, (me + 1) % TILES

    def halo_pair(ref, k):
        up = pltpu.make_async_remote_copy(
            src_ref=ref.at[2], dst_ref=ref.at[0],
            send_sem=halo_s.at[2 * k], recv_sem=halo_r.at[2 * k],
            device_id=(clip, high_peer), device_id_type=MESH)
        down = pltpu.make_async_remote_copy(
            src_ref=ref.at[1], dst_ref=ref.at[3],
            send_sem=halo_s.at[2 * k + 1], recv_sem=halo_r.at[2 * k + 1],
            device_id=(clip, low_peer), device_id_type=MESH)
        return up, down

    def put_halo(ref, y_ref, f):
        put_row(y_ref, f, 0, jnp.where(me > 0, ref[0, f].astype(F32), 0.0).astype(BF16))
        put_row(y_ref, f, 3, jnp.where(me < TILES - 1, ref[3, f].astype(F32), 0.0).astype(BF16))

    def x_pair(c):
        at = pl.ds(CHUNK * c, CHUNK)
        up = pltpu.make_async_remote_copy(
            src_ref=x4.at[2, at], dst_ref=x4.at[0, at],
            send_sem=x_s.at[2 * c], recv_sem=x_r.at[2 * c],
            device_id=(clip, high_peer), device_id_type=MESH)
        down = pltpu.make_async_remote_copy(
            src_ref=x4.at[1, at], dst_ref=x4.at[3, at],
            send_sem=x_s.at[2 * c + 1], recv_sem=x_r.at[2 * c + 1],
            device_id=(clip, low_peer), device_id_type=MESH)
        return up, down

    def rw_arrived(i):
        src = tile_peer(i)
        rw_copy(src, src, src, src).wait_recv()

    own_rw.wait()
    loop(15, rw_arrived)
    for i in range(C // 16):
        rows = slice(16 * i, 16 * i + 16)
        slots = jnp.concatenate(
            [rrw[:, :, h, rows, :].reshape(512, W) for h in range(2)], axis=1)
        got = jnp.dot(pick[...], slots, preferred_element_type=F32).astype(BF16)
        got = got.reshape(FRAMES, 16, 2 * W)
        xg4[1, :, rows, :] = got[:, :, :W]
        xg4[2, :, rows, :] = got[:, :, W:]
    halo = halo_pair(xg4, 0)
    for copy in halo:
        copy.start()
    loop(15 - EARLY, lambda i: start_in(i + EARLY))

    def put_own(f):
        for h in range(2):
            put_row(yg, f, 1 + h, xg4[1 + h, f])

    loop(FRAMES, put_own)

    def conv(kernel_ref, y_ref, first, each):
        c1[...] = jnp.zeros_like(c1)
        c2[...] = jnp.zeros_like(c2)

        def frame(f, one, two):
            p = jnp.dot(kernel_ref[...], y_ref[f], preferred_element_type=F32)
            if first is not None:
                one, two = jnp.where(f == FRAMES - 1, 0.0, one), jnp.where(f == FRAMES - 1, 0.0, two)
            return p[2 * C:] + one, p[C:2 * C] + two, p[:C]

        if first is not None:
            zero = jnp.zeros((C, 2 * W), F32)
            _, one, two = frame((first + 2) % FRAMES, zero, zero)
            _, one, two = frame((first + 1) % FRAMES, one, two)
            c1[...] = one
            c2[...] = two

        def body(i):
            one, two = c1[...], c2[...]
            for k in range(UNROLL):
                step = i * UNROLL + k
                f = step
                if first is not None:
                    f = (first + FRAMES - f) % FRAMES
                else:
                    f = FRAMES - 1 - f
                value, one, two = frame(f, one, two)
                each(step, f, value.astype(BF16))
            c1[...] = one
            c2[...] = two

        loop(FRAMES // UNROLL, body)

    def keep(step, f, g):
        gm[f] = g

    def first(f):
        for h in range(2):
            v = norm_silu(rin[f, h].astype(F32), g1c[...]).astype(BF16)
            x4[1 + h, f] = v
            put_row(yin, f, 1 + h, v)

    own_in.wait()
    first(me)

    def arrived(i):
        src = tile_peer(i)
        in_copy(src, src, src, src).wait_recv()
        first(src)

    loop(15, arrived)

    def send_x(c):
        for copy in x_pair(c):
            copy.start()

    loop(FRAMES // CHUNK, send_x)

    for copy in halo:
        copy.wait()
    loop(FRAMES, lambda f: put_halo(xg4, yg, f))
    conv(k2t, yg, None, keep)

    def mid(f, h):
        for row in range(2):
            lanes = slice(row * W, (row + 1) * W)
            v, g = mid_both(gm[f, :, lanes].astype(F32), h[:, lanes].astype(F32), g2c[...])
            act[f + 2, :, lanes] = v.astype(BF16)
            g = g.astype(BF16)
            xh4[1 + row, f] = g
            gh[f, :, lanes] = g
            put_row(yh, f, 1 + row, g)

    c1[...] = jnp.zeros_like(c1)
    c2[...] = jnp.zeros_like(c2)

    def chunk(c):
        for copy in x_pair(c):
            copy.wait()
        for k in range(CHUNK):
            put_halo(x4, yin, c * CHUNK + k)
        one, two = c1[...], c2[...]
        for k in range(CHUNK):
            f = c * CHUNK + k
            p = jnp.dot(k1f[...], yin[f], preferred_element_type=F32)
            mid(f, (p[2 * C:] + one).astype(BF16))
            one = p[C:2 * C] + two
            two = p[:C]
        c1[...] = one
        c2[...] = two

    loop(FRAMES // CHUNK, chunk)
    halo = halo_pair(xh4, 1)
    for copy in halo:
        copy.start()

    mine, other = core * 64, (1 - core) * 64

    def weight(n, left, y_ref):
        def body(i):
            total = w[n, :, :TAPS]
            for k in range(4):
                f = i * 4 + k
                rows = left(f)
                total = total + lax.dot_general(
                    rows, y_ref[f], (((1,), (1,)), ((), ())), preferred_element_type=F32)
            w[n, :, :TAPS] = total

        loop(FRAMES // 4, body)

        def pack(i):
            rows = w[n, pl.ds(pl.multiple_of(16 * i, 16), 16), :]
            for j in range(7):
                piece = rows[:, 128 * j:128 * (j + 1)]
                bb[n, 7 * i + j] = piece
                sb[n, 7 * i + j] = piece.astype(BF16)

        loop(18, pack)

    def s0_copy(n, piece):
        return pltpu.make_async_remote_copy(
            src_ref=sb.at[n, pl.ds(other + 4 * piece, 4)], dst_ref=r0.at[n, pl.ds(4 * piece, 4)],
            send_sem=s0_s.at[n, piece], recv_sem=s0_r.at[n, piece],
            device_id=(clip, sibling), device_id_type=MESH)

    def s1_copy(n, piece, slot_at, peer):
        return pltpu.make_async_remote_copy(
            src_ref=s1b.at[n, pl.ds(4 * piece, 4)], dst_ref=r1.at[n, slot_at],
            send_sem=s1_s.at[n, piece], recv_sem=s1_r.at[n, slot_at],
            device_id=(peer, me), device_id_type=MESH)

    def s2_copy(to, slot_at):
        return pltpu.make_async_remote_copy(
            src_ref=c16, dst_ref=r2.at[slot_at],
            send_sem=s2_s.at[to], recv_sem=s2_r.at[slot_at],
            device_id=(clip, 2 * to + core), device_id_type=MESH)

    def a1_copy(at, to):
        piece = res_ref.at[16 * core + at]
        return pltpu.make_async_remote_copy(
            src_ref=piece, dst_ref=piece,
            send_sem=a1_s.at[to], recv_sem=a1_r.at[at],
            device_id=(to, me), device_id_type=MESH)

    def a0_copy(half, at):
        piece = res_ref.at[16 * half + at]
        return pltpu.make_async_remote_copy(
            src_ref=piece, dst_ref=piece, send_sem=a0_s.at[at], recv_sem=a0_r.at[at],
            device_id=(clip, sibling), device_id_type=MESH)

    def sum_pair(n):
        loop(16, lambda i: s0_copy(n, clip_peer(i)).start())

    def sum_clips(n):
        def piece_of(p):
            s0_copy(n, p).wait()
            return (bb[n, pl.ds(mine + 4 * p, 4)]
                    + r0[n, pl.ds(4 * p, 4)].astype(F32)).astype(BF16)

        def add(i):
            p = clip_peer(i)
            s1b[n, pl.ds(4 * p, 4)] = piece_of(p)
            s1_copy(n, p, clip, p).start()

        loop(15, add)
        r1[n, clip] = piece_of(clip)

    def sum_z():
        for n in range(2):
            loop(15, lambda i: s1_copy(n, clip_peer(i), clip_peer(i), clip_peer(i)).wait())

            def add(i):
                total = r1[n, 0, i].astype(F32)
                for p in range(1, CLIPS):
                    total = total + r1[n, p, i].astype(F32)
                c16[4 * n + i] = total.astype(BF16)

            loop(4, add)
        loop(7, lambda i: s2_copy(z_of(i), z).start())
        r2[z] = c16[...]

    def spread_clips():
        loop(7, lambda i: s2_copy(z_of(i), z_of(i)).wait())
        total = r2[0].astype(F32)
        for p in range(1, 8):
            total = total + r2[p].astype(F32)
        res_ref[16 * core + clip] = total.astype(BF16)
        loop(15, lambda i: a1_copy(clip, clip_peer(i)).start())
        a0_copy(core, clip).start()

    def spread_pair():
        def forward(i):
            p = clip_peer(i)
            a1_copy(p, p).wait_recv()
            a0_copy(core, p).start()

        loop(15, forward)

    def finish_sum():
        loop(15, lambda i: a1_copy(clip, clip_peer(i)).wait_send())
        loop(16, lambda i: a0_copy(1 - core, i).wait_recv())
        loop(16, lambda i: a0_copy(core, i).wait_send())

    weight(0, lambda f: jnp.concatenate([gh[f + 2], gh[f + 1], gh[f]], axis=0), yin)
    sum_pair(0)
    weight(1, lambda f: jnp.concatenate([act[f], act[f + 1], act[f + 2]], axis=0), yg)
    sum_pair(1)
    sum_clips(0)
    for copy in halo:
        copy.wait()
    loop(FRAMES, lambda f: put_halo(xh4, yh, f))
    sum_clips(1)

    def f_copy(f, dst_rows, slot_at, peer):
        return pltpu.make_async_remote_copy(
            src_ref=fb.at[f], dst_ref=out_ref.at[pl.ds(2 * dst_rows, 2)],
            send_sem=f_s.at[f], recv_sem=f_r.at[slot_at],
            device_id=(clip, peer), device_id_type=MESH)

    own_out = pltpu.make_async_copy(fb.at[me], out_ref.at[pl.ds(2 * me, 2)], loc.at[2])

    def back_in(step, f, g):
        for row in range(2):
            v = norm_backward(
                g[:, row * W:(row + 1) * W].astype(F32), rin[f, row].astype(F32), g1c[...])
            fb[f, row] = (xg4[1 + row, f].astype(F32) + v).astype(BF16)

        @pl.when((f != me) & (step < FRAMES - HELD))
        def _():
            f_copy(f, me, me, f).start()

        @pl.when(f == me)
        def _():
            own_out.start()

    conv(k1t, yh, (me + 8) % FRAMES, back_in)

    sum_z()

    def send_held(i):
        f = (me + 8 + HELD - i) % FRAMES

        @pl.when(f != me)
        def _():
            f_copy(f, me, me, f).start()

    loop(HELD, send_held)
    spread_clips()
    spread_pair()
    finish_sum()

    own_out.wait()

    def drain(i):
        peer = tile_peer(i)
        f_copy(peer, peer, peer, peer).wait_recv()
        f_copy(peer, me, me, peer).wait_send()
        in_copy(peer, me, me, peer).wait_send()
        rw_copy(peer, me, me, peer).wait_send()

    loop(15, drain)


def unpack(scale, p_ref, o1_ref, o2_ref, s_ref):
    for n, o_ref in enumerate((o1_ref, o2_ref)):
        for t in range(126):
            i, j = divmod(t, 7)
            s_ref[16 * i:16 * (i + 1), 128 * j:128 * (j + 1)] = (
                p_ref[t // 4, 4 * n + t % 4].astype(F32) * scale)
        for a in range(3):
            for i in range(9):
                block = s_ref[a * C:(a + 1) * C, i * C:(i + 1) * C]
                if n == 0:
                    o_ref[a * 9 + i] = block
                else:
                    o_ref[a * 9 + 8 - i] = jnp.transpose(block)


def local(
    decoder_input, reward_grad, reward_owner, scored_frame,
    first_gain, second_gain, first_kernel, second_kernel,
):
    vmem = pl.BlockSpec(memory_space=pltpu.VMEM)
    hbm = pl.BlockSpec(memory_space=pl.ANY)
    dma = pltpu.SemaphoreType.DMA
    feature, packed = pl.pallas_call(
        kernel,
        out_shape=(
            jax.ShapeDtypeStruct((32, C, W), BF16),
            jax.ShapeDtypeStruct((32, 8, 16, 128), BF16),
        ),
        in_specs=[hbm, hbm] + [vmem] * 6,
        out_specs=(hbm, vmem),
        scratch_shapes=[
            pltpu.VMEM((16, 2, C, W), BF16),
            pltpu.VMEM((16, 2, 2, C, W), BF16),
            pltpu.VMEM((3 * C, TAPS), BF16),
            pltpu.VMEM((3 * C, TAPS), BF16),
            pltpu.VMEM((3 * C, TAPS), BF16),
            pltpu.VMEM((C, W), F32),
            pltpu.VMEM((C, W), F32),
            pltpu.VMEM((256, 512), BF16),
            pltpu.VMEM((4, 16, C, W), BF16),
            pltpu.VMEM((4, 16, C, W), BF16),
            pltpu.VMEM((4, 16, C, W), BF16),
            pltpu.VMEM((16, TAPS, 2 * W), BF16),
            pltpu.VMEM((16, TAPS, 2 * W), BF16),
            pltpu.VMEM((16, TAPS, 2 * W), BF16),
            pltpu.VMEM((16, C, 2 * W), BF16),
            pltpu.VMEM((18, C, 2 * W), BF16),
            pltpu.VMEM((18, C, 2 * W), BF16),
            pltpu.VMEM((C, 2 * W), F32),
            pltpu.VMEM((C, 2 * W), F32),
            pltpu.VMEM((16, 2, C, W), BF16),
            pltpu.VMEM((2, 3 * C, PADDED), F32),
            pltpu.VMEM((2, 128, 16, 128), F32),
            pltpu.VMEM((2, 128, 16, 128), BF16),
            pltpu.VMEM((2, 64, 16, 128), BF16),
            pltpu.VMEM((2, 64, 16, 128), BF16),
            pltpu.VMEM((2, 16, 4, 16, 128), BF16),
            pltpu.VMEM((8, 16, 128), BF16),
            pltpu.VMEM((8, 8, 16, 128), BF16),
            dma((16,)), dma((16,)), dma((16,)), dma((16,)), dma((3,)),
            dma((4,)), dma((4,)), dma((8,)), dma((8,)), dma((16,)), dma((16,)),
            dma((2, 16)), dma((2, 16)), dma((2, 16)), dma((2, 16)), dma((8,)), dma((8,)),
            dma((16,)), dma((16,)), dma((16,)), dma((16,)),
        ],
        compiler_params=pltpu.CompilerParams(
            collective_id=0, has_side_effects=True, vmem_limit_bytes=60 * 2**20),
    )(
        decoder_input[0, 0],
        reward_grad[0],
        reward_owner[0].reshape(1, 16),
        scored_frame,
        first_gain.reshape(1, C),
        second_gain.reshape(1, C),
        first_kernel.reshape(27, C, C),
        second_kernel.reshape(27, C, C),
    )
    first_total, second_total = pl.pallas_call(
        functools.partial(unpack, 1.0 / 1024.0),
        out_shape=(jax.ShapeDtypeStruct((27, C, C), F32),) * 2,
        in_specs=[vmem],
        out_specs=(vmem, vmem),
        scratch_shapes=[pltpu.VMEM((3 * C, PADDED), F32)],
        compiler_params=pltpu.CompilerParams(vmem_limit_bytes=32 * 2**20),
    )(packed)
    shape = (3, 3, 3, C, C)
    return feature[None, None], first_total.reshape(shape), second_total.reshape(shape)


def solution(mesh):
    in_specs = (
        P("clip", "tile", None, None, None),
        P("clip", "tile", None, None, None),
        P("clip", None, None),
        P("clip", None),
        P(),
        P(),
        P(),
        P(),
    )
    out_specs = (P("clip", "tile", None, None, None), P(), P())
    return jax.shard_map(local, mesh=mesh, in_specs=in_specs, out_specs=out_specs, check_vma=False)
```
